32 devices in a mesh: group: 2 (over y), sector: 4 (over z), op: 2 (over x), half: 2 (over core).
Axes of the slice: x: 2, y: 2, z: 4, core: 2. Of those that a mesh axis runs over, the one named last changes fastest.
Arguments:
- wavefunction: bfloat16 [24, 512, 512], P(('group', 'sector'), 'half'), parts along dimension 0, may hold values from -6 to 6
- left_env: bfloat16 [4, 24, 512, 512], P('op', ('group', 'sector'), 'half'), parts along dimension 1, may hold values from -0.25 to 0.25
- right_env: bfloat16 [4, 24, 512, 512], P('op', ('group', 'sector'), 'half'), parts along dimension 1, may hold values from -0.25 to 0.25
- source: int32 [4, 24], P(None, 'group'), parts along dimension 1, may hold values from 0 to 11, as said below
- left_dims: int32 [24], P('group'), parts along dimension 0, may hold values from 64 to 512
- right_dims: int32 [24], P('group'), parts along dimension 0, may hold values from 64 to 512
Outputs:
- sigma_product: bfloat16 [24, 512, 512], P(('group', 'sector'), 'half', 'op'), parts along dimension 0
The draws below stay inside these ranges and needn't reach their ends.
There are 2 independent parts, one for each index of `group`. The reference program is written for one: setup_inputs(seed, part) draws one part's arguments, and reference() takes and returns one part's arrays. A program takes and returns all parts, laid end to end along the dimension named above; each array names one. Nothing has to cross between parts.
Inputs may be any that keep to these rules, and one draw needn't show every extreme that they name: For every op index o and sector index j, the sources source[k, t] over the 2 pairs of o and the 3 targets of j lie at most 2 in any one sector index (source // 3), and exactly 2 in some.
All inputs are finite; a program needn't handle non-finite values.
Results may differ from the reference program's by a relative error of at most 0.0049.
Values may be sent and summed in bfloat16 or wider, within the bound.
No kernel may reach another device: no remote copies, remote signals or barrier semaphores. Data moves between devices by JAX's collectives and lax.ppermute only.
A program may use at most 64 MiB of HBM per device.

```python
import jax
import jax.numpy as jnp
from jax import lax

BLK = 512
K_DEV = 2
S_DEV = 3
K = 4
S = 12
CAP = 2
N_SECTOR = 4
N_OP = 2


def draw_source(key, part):
    key = jax.random.fold_in(key, 11)
    needed = K_DEV * S_DEV
    keys = jax.random.split(key, N_OP * N_SECTOR)

    def one_block(block_key):
        perm_key, slot_key = jax.random.split(block_key)
        shards = jnp.concatenate([jax.random.permutation(jax.random.fold_in(perm_key, c), N_SECTOR) for c in range(CAP)])
        shards = shards[:needed]
        slots = jax.random.randint(slot_key, (needed,), 0, S_DEV)
        return shards * S_DEV + slots
    values = jax.vmap(one_block)(keys)
    values = values.reshape(N_OP, N_SECTOR, K_DEV, S_DEV).transpose(0, 2, 1, 3).reshape(K, S)
    return values.astype(jnp.int32)


def dims_common(key):
    first_key, second_key = jax.random.split(key)
    values = jax.random.randint(first_key, (S,), BLK // 8, BLK + 1)
    spot = jax.random.randint(second_key, (), 0, S)
    return jnp.where(jnp.arange(S) == spot, BLK, values).astype(jnp.int32)


def draw_left_dims(key, part):
    key = jax.random.fold_in(key, 3)
    return dims_common(key)


def draw_right_dims(key, part):
    key = jax.random.fold_in(key, 5)
    return dims_common(key)


def block_scale(key, dims, cuts, smallest, top_value):
    gain, own = 1.0, jax.random.fold_in(key, 6)
    for axis_at, blocks in cuts:
        draws = jnp.exp(jax.random.uniform(jax.random.fold_in(own, axis_at), (blocks,), jnp.float32, smallest / len(cuts), top_value / len(cuts)))
        gain = gain * jnp.repeat(draws, dims[axis_at] // blocks).reshape([-1 if axis == axis_at else 1 for axis in range(len(dims))])
    return gain


def normal_values(rng, shape, scale, limit, cuts=(), held_as=jnp.bfloat16):
    loudness = block_scale(rng, shape, cuts, -0.22, 0.18) if cuts else 1.0
    entries = jax.random.normal(rng, shape, jnp.float32) * scale * loudness
    return jnp.minimum(jnp.maximum(entries, -limit), limit).astype(held_as)


def setup_inputs(seed: int = 0, part: int = 0) -> dict:
    key_of = jax.random.split(jax.random.key(seed), 7)
    own_keys = jax.random.split(jax.random.fold_in(key_of[6], part), 7)
    return {
        "wavefunction": normal_values(own_keys[0], (S, BLK, BLK), 1.0, 6.0, ((0, 4), (1, 2))),
        "left_env": normal_values(own_keys[1], (K, S, BLK, BLK), BLK ** -0.5, 0.25, ((0, 2), (1, 4), (2, 2))),
        "right_env": normal_values(own_keys[2], (K, S, BLK, BLK), BLK ** -0.5, 0.25, ((0, 2), (1, 4), (2, 2))),
        "source": draw_source(jax.random.fold_in(jax.random.fold_in(key_of[6], part), 71), part),
        "left_dims": draw_left_dims(jax.random.fold_in(jax.random.fold_in(key_of[6], part), 71), part),
        "right_dims": draw_right_dims(jax.random.fold_in(jax.random.fold_in(key_of[6], part), 71), part),
    }


def reference(wavefunction, left_env, right_env, source, left_dims, right_dims):
    row_index = jnp.arange(BLK, dtype=jnp.int32)
    left_live = row_index[None, :] < left_dims[:, None]
    right_live = row_index[None, :] < right_dims[:, None]
    live_mask = left_live[:, :, None] & right_live[:, None, :]
    masked = jnp.where(live_mask, wavefunction, jnp.zeros((), wavefunction.dtype))

    def one_target(target):
        def one_pair(total, pair_index):
            anchor = source[pair_index, target]
            right_part = jnp.dot(masked[anchor], right_env[pair_index, target].T, preferred_element_type=jnp.float32).astype(jnp.bfloat16)
            return total + jnp.dot(left_env[pair_index, target], right_part, preferred_element_type=jnp.float32), None

        total, _ = lax.scan(one_pair, jnp.zeros((BLK, BLK), jnp.float32), jnp.arange(K, dtype=jnp.int32))
        return jnp.where(live_mask[target], total, jnp.zeros((), jnp.float32)).astype(jnp.bfloat16)

    return lax.map(one_target, jnp.arange(S, dtype=jnp.int32))
```

```python
import functools

import jax
import jax.numpy as jnp
from jax import lax
from jax.experimental import pallas as pl
from jax.experimental.pallas import tpu as pltpu
from jax.sharding import PartitionSpec as P

BF16 = jnp.bfloat16
F32 = jnp.float32


def general(wavefunction, left_env, right_env, source, left_dims, right_dims):
    sec_local, half_rows, blk_cols = wavefunction.shape
    pair_local = left_env.shape[0]
    needed = pair_local * sec_local
    sector_count = lax.axis_size("sector")
    sector_me = lax.axis_index("sector")
    op_me = lax.axis_index("op")
    half_me = lax.axis_index("half")
    places = sector_me * sec_local + jnp.arange(sec_local, dtype=jnp.int32)
    row_ids = half_me * half_rows + jnp.arange(half_rows, dtype=jnp.int32)
    col_ids = jnp.arange(blk_cols, dtype=jnp.int32)
    left_live = jnp.take(left_dims, places)
    right_live = jnp.take(right_dims, places)
    live_mask = (row_ids[None, :, None] < left_live[:, None, None]) & (
        col_ids[None, None, :] < right_live[:, None, None]
    )
    masked = jnp.where(live_mask, wavefunction, jnp.zeros((), wavefunction.dtype))
    wanted = lax.dynamic_slice(source, (op_me * pair_local, 0), (pair_local, source.shape[1]))
    wanted = (
        wanted.reshape(pair_local, sector_count, sec_local)
        .transpose(1, 0, 2)
        .reshape(sector_count, needed)
    )
    own_needs = lax.dynamic_index_in_dim(wanted, sector_me, 0, keepdims=False)
    capacity = -(-needed // sector_count)
    holders = wanted // sec_local
    is_mine = (holders == sector_me).astype(jnp.int32)
    earlier_hits = jnp.cumsum(is_mine, axis=1) - is_mine
    slot_ids = jnp.arange(capacity, dtype=jnp.int32)
    pick_mask = (is_mine[:, :, None] == 1) & (earlier_hits[:, :, None] == slot_ids[None, None, :])
    local_slot = jnp.sum(jnp.where(pick_mask, (wanted % sec_local)[:, :, None], 0), axis=1)
    outgoing = jnp.take(masked, local_slot.reshape(-1), axis=0).reshape(
        sector_count, capacity, half_rows, blk_cols
    )
    incoming = lax.all_to_all(outgoing, "sector", split_axis=0, concat_axis=0, tiled=True)
    owners = own_needs // sec_local
    same_owner = owners[:, None] == owners[None, :]
    order_ids = jnp.arange(needed, dtype=jnp.int32)
    earlier = order_ids[None, :] < order_ids[:, None]
    rank_of = jnp.sum((same_owner & earlier).astype(jnp.int32), axis=1)
    fetched = jnp.take(
        incoming.reshape(sector_count * capacity, half_rows, blk_cols),
        owners * capacity + rank_of,
        axis=0,
    )
    right_rows = right_env.reshape(needed, right_env.shape[2], blk_cols)
    right_part = jnp.einsum(
        "nab,ncb->nac",
        lax.all_gather(fetched, "half", axis=1, tiled=True),
        right_rows,
        preferred_element_type=F32,
    ).astype(BF16)
    right_part = right_part.reshape(pair_local, sec_local, right_part.shape[1], right_part.shape[2])
    partial_sum = jnp.einsum(
        "ksrc,kscj->srj",
        left_env,
        lax.all_gather(right_part, "half", axis=3, tiled=True),
        preferred_element_type=F32,
    )
    summed = lax.psum_scatter(partial_sum, "op", scatter_dimension=2, tiled=True)
    col_width = summed.shape[2]
    out_cols = op_me * col_width + jnp.arange(col_width, dtype=jnp.int32)
    out_mask = (row_ids[None, :, None] < left_live[:, None, None]) & (
        out_cols[None, None, :] < right_live[:, None, None]
    )
    return jnp.where(out_mask, summed, jnp.zeros((), F32)).astype(BF16)


def sigma_kernel(
    sizes, me, source, left_dims, right_dims, *refs
):
    pairs, secs, half_rows, blk = sizes
    quarter = half_rows // 2
    own, own_far = refs[0:2]
    slabs = (refs[2:6], refs[6:10], refs[10:14])
    left, right, right_far = refs[14:17]
    send, keep = refs[17:19]
    m_buf, r_buf, l_buf, m_sem, r_sem, l_sem = refs[19:25]
    z, o, h = me[0], me[1], me[2]

    def slot(n):
        k, t = n // secs, n % secs
        src = source[o * pairs + k, z * secs + t]
        holder = src // secs
        return k, t, src, holder ^ z, src - holder * secs

    for n in range(pairs * secs):
        k, t, src, kind, local = slot(n)
        rows_mine = pl.multiple_of(h * half_rows, half_rows)
        rows_far = pl.multiple_of((1 - h) * half_rows, half_rows)

        @pl.when(kind == 0)
        def _():
            pltpu.make_async_copy(own.at[local], m_buf.at[n, pl.ds(rows_mine, half_rows)], m_sem.at[n]).start()
            pltpu.make_async_copy(own_far.at[local], m_buf.at[n, pl.ds(rows_far, half_rows)], m_sem.at[n]).start()

        for s in range(3):
            @pl.when(kind == s + 1)
            def _():
                for piece, (base, at) in enumerate(
                    ((rows_mine, o), (rows_mine, 1 - o), (rows_far, o), (rows_far, 1 - o))
                ):
                    first = pl.multiple_of(base + at * quarter, quarter)
                    pltpu.make_async_copy(
                        slabs[s][piece].at[local], m_buf.at[n, pl.ds(first, quarter)], m_sem.at[n]
                    ).start()

        at_mine = pl.multiple_of((h ^ o) * half_rows, half_rows)
        at_far = pl.multiple_of((1 - (h ^ o)) * half_rows, half_rows)
        pltpu.make_async_copy(right.at[k, t], r_buf.at[n, pl.ds(at_mine, half_rows)], r_sem.at[n]).start()
        pltpu.make_async_copy(right_far.at[k, t], r_buf.at[n, pl.ds(at_far, half_rows)], r_sem.at[n]).start()
        pltpu.make_async_copy(left.at[k, t], l_buf.at[n], l_sem.at[n]).start()

    def one_slot(n):
        k, t, src, kind, local = slot(n)
        pltpu.make_async_copy(m_buf.at[n], m_buf.at[n], m_sem.at[n]).wait()
        pltpu.make_async_copy(r_buf.at[n], r_buf.at[n], r_sem.at[n]).wait()
        pltpu.make_async_copy(l_buf.at[n], l_buf.at[n], l_sem.at[n]).wait()
        col = lax.broadcasted_iota(jnp.int32, (1, blk), 1)
        col_live = (col < right_dims[src]).astype(F32).astype(BF16)
        block = m_buf[n] * col_live
        part = lax.dot_general(block, r_buf[n], (((1,), (1,)), ((), ())), preferred_element_type=F32)
        row = lax.broadcasted_iota(jnp.int32, (blk, 1), 0)
        part = jnp.where(row < left_dims[src], part, 0.0).astype(BF16)
        return lax.dot_general(l_buf[n], part, (((1,), (0,)), ((), ())), preferred_element_type=F32)

    for t in range(secs):
        total = one_slot(t)
        for k in range(1, pairs):
            total = total + one_slot(k * secs + t)
        keep[t] = total[:, : blk // 2]
        send[t] = total[:, blk // 2 :].astype(BF16)


def swap(x, axis):
    return lax.ppermute(x, axis, [(0, 1), (1, 0)])


def four_by_two(wavefunction, left_env, right_env, source, left_dims, right_dims):
    secs, half_rows, blk = wavefunction.shape
    pairs = left_env.shape[0]
    quarter = half_rows // 2
    z, o, h = lax.axis_index("sector"), lax.axis_index("op"), lax.axis_index("half")
    me = jnp.stack([z, o, h]).astype(jnp.int32)
    share = lax.dynamic_slice_in_dim(wavefunction, o * quarter, quarter, axis=1)
    slabs = []
    for kind in (1, 2, 3):
        slabs.append(lax.ppermute(share, "sector", [(i, i ^ kind) for i in range(4)]))
    own_far = swap(wavefunction, "half")
    right_far = swap(right_env, "half")
    pieces = []
    for slab in slabs:
        other = swap(slab, "op")
        pieces += [slab, other, swap(slab, "half"), swap(other, "half")]
    smem = pl.BlockSpec(memory_space=pltpu.SMEM)
    any_spec = pl.BlockSpec(memory_space=pl.ANY)
    vmem = pl.BlockSpec(memory_space=pltpu.VMEM)
    needed = pairs * secs
    send, keep = pl.pallas_call(
        functools.partial(sigma_kernel, (pairs, secs, half_rows, blk)),
        out_shape=(
            jax.ShapeDtypeStruct((secs, half_rows, blk // 2), BF16),
            jax.ShapeDtypeStruct((secs, half_rows, blk // 2), F32),
        ),
        in_specs=[smem] * 4 + [any_spec] * 17,
        out_specs=(vmem, vmem),
        scratch_shapes=[
            pltpu.VMEM((needed, blk, blk), BF16),
            pltpu.VMEM((needed, blk, blk), BF16),
            pltpu.VMEM((needed, half_rows, blk), BF16),
            pltpu.SemaphoreType.DMA((needed,)),
            pltpu.SemaphoreType.DMA((needed,)),
            pltpu.SemaphoreType.DMA((needed,)),
        ],
        compiler_params=pltpu.CompilerParams(vmem_limit_bytes=40 * 1024 * 1024),
        name="sigma_slots",
    )(me, source, left_dims, right_dims, wavefunction, own_far, *pieces, left_env, right_env, right_far)
    total = keep + swap(send, "op").astype(F32)
    places = z * secs + jnp.arange(secs, dtype=jnp.int32)
    row_ids = h * half_rows + jnp.arange(half_rows, dtype=jnp.int32)
    col_ids = o * (blk // 2) + jnp.arange(blk // 2, dtype=jnp.int32)
    live = (row_ids[None, :, None] < jnp.take(left_dims, places)[:, None, None]) & (
        col_ids[None, None, :] < jnp.take(right_dims, places)[:, None, None]
    )
    return jnp.where(live, total, 0.0).astype(BF16)


def solution(mesh):
    shape = mesh.shape
    fits = (shape["sector"], shape["op"], shape["half"]) == (4, 2, 2)
    return jax.shard_map(
        four_by_two if fits else general,
        mesh=mesh,
        in_specs=(
            P(("group", "sector"), "half", None),
            P("op", ("group", "sector"), "half", None),
            P("op", ("group", "sector"), "half", None),
            P(None, "group"),
            P("group"),
            P("group"),
        ),
        out_specs=P(("group", "sector"), "half", "op"),
        check_vma=False,
    )
```

```python
import functools

import jax
import jax.numpy as jnp
from jax import lax
from jax.experimental import pallas as pl
from jax.experimental.pallas import tpu as pltpu
from jax.sharding import PartitionSpec as P

BF16 = jnp.bfloat16
F32 = jnp.float32
VMEM_EARLY = 48 * 1024 * 1024
VMEM_LATE = 56 * 1024 * 1024


def general(wavefunction, left_env, right_env, source, left_dims, right_dims):
    sec_local, half_rows, blk_cols = wavefunction.shape
    pair_local = left_env.shape[0]
    needed = pair_local * sec_local
    sector_count = lax.axis_size("sector")
    sector_me = lax.axis_index("sector")
    op_me = lax.axis_index("op")
    half_me = lax.axis_index("half")
    places = sector_me * sec_local + jnp.arange(sec_local, dtype=jnp.int32)
    row_ids = half_me * half_rows + jnp.arange(half_rows, dtype=jnp.int32)
    col_ids = jnp.arange(blk_cols, dtype=jnp.int32)
    left_live = jnp.take(left_dims, places)
    right_live = jnp.take(right_dims, places)
    live_mask = (row_ids[None, :, None] < left_live[:, None, None]) & (
        col_ids[None, None, :] < right_live[:, None, None]
    )
    masked = jnp.where(live_mask, wavefunction, jnp.zeros((), wavefunction.dtype))
    wanted = lax.dynamic_slice(source, (op_me * pair_local, 0), (pair_local, source.shape[1]))
    wanted = (
        wanted.reshape(pair_local, sector_count, sec_local)
        .transpose(1, 0, 2)
        .reshape(sector_count, needed)
    )
    own_needs = lax.dynamic_index_in_dim(wanted, sector_me, 0, keepdims=False)
    capacity = -(-needed // sector_count)
    holders = wanted // sec_local
    is_mine = (holders == sector_me).astype(jnp.int32)
    earlier_hits = jnp.cumsum(is_mine, axis=1) - is_mine
    slot_ids = jnp.arange(capacity, dtype=jnp.int32)
    pick_mask = (is_mine[:, :, None] == 1) & (earlier_hits[:, :, None] == slot_ids[None, None, :])
    local_slot = jnp.sum(jnp.where(pick_mask, (wanted % sec_local)[:, :, None], 0), axis=1)
    outgoing = jnp.take(masked, local_slot.reshape(-1), axis=0).reshape(
        sector_count, capacity, half_rows, blk_cols
    )
    incoming = lax.all_to_all(outgoing, "sector", split_axis=0, concat_axis=0, tiled=True)
    owners = own_needs // sec_local
    same_owner = owners[:, None] == owners[None, :]
    order_ids = jnp.arange(needed, dtype=jnp.int32)
    earlier = order_ids[None, :] < order_ids[:, None]
    rank_of = jnp.sum((same_owner & earlier).astype(jnp.int32), axis=1)
    fetched = jnp.take(
        incoming.reshape(sector_count * capacity, half_rows, blk_cols),
        owners * capacity + rank_of,
        axis=0,
    )
    right_rows = right_env.reshape(needed, right_env.shape[2], blk_cols)
    right_part = jnp.einsum(
        "nab,ncb->nac",
        lax.all_gather(fetched, "half", axis=1, tiled=True),
        right_rows,
        preferred_element_type=F32,
    ).astype(BF16)
    right_part = right_part.reshape(pair_local, sec_local, right_part.shape[1], right_part.shape[2])
    partial_sum = jnp.einsum(
        "ksrc,kscj->srj",
        left_env,
        lax.all_gather(right_part, "half", axis=3, tiled=True),
        preferred_element_type=F32,
    )
    summed = lax.psum_scatter(partial_sum, "op", scatter_dimension=2, tiled=True)
    col_width = summed.shape[2]
    out_cols = op_me * col_width + jnp.arange(col_width, dtype=jnp.int32)
    out_mask = (row_ids[None, :, None] < left_live[:, None, None]) & (
        out_cols[None, None, :] < right_live[:, None, None]
    )
    return jnp.where(out_mask, summed, jnp.zeros((), F32)).astype(BF16)


def kinds_of(source, me, pairs, secs, op):
    z = me[0]
    found = []
    for n in range(pairs * secs):
        src = source[op * pairs + n // secs, z * secs + n % secs]
        holder = src // secs
        found.append((holder ^ z, src - holder * secs, src))
    return found


def ranked(slots, kind, rank):
    slot, local, source = jnp.int32(-1), jnp.int32(0), jnp.int32(0)
    seen = jnp.int32(0)
    for n, (k, b, s) in enumerate(slots):
        hit = (k == kind) & (seen == rank)
        slot = jnp.where(hit, n, slot)
        local = jnp.where(hit, b, local)
        source = jnp.where(hit, s, source)
        seen = seen + (k == kind).astype(jnp.int32)
    return slot, local, source


def plan_kernel(sizes, me, source, left, right, left_out, right_out, picks, sem):
    pairs, secs, half_rows, blk = sizes
    quarter = half_rows // 2
    o = me[1]
    mine = kinds_of(source, me, pairs, secs, o)
    theirs = kinds_of(source, me, pairs, secs, 1 - o)
    copies = []
    for j in range(2):
        n = jnp.maximum(ranked(mine, 3, j)[0], 0)
        k, t = n // secs, n % secs
        copies.append(pltpu.make_async_copy(right.at[k, t], right_out.at[j], sem.at[len(copies)]))
        for part in range(2):
            first = pl.multiple_of(part * half_rows + (1 - o) * quarter, quarter)
            copies.append(
                pltpu.make_async_copy(
                    left.at[k, t, :, pl.ds(first, quarter)],
                    left_out.at[j, :, pl.ds(part * quarter, quarter)],
                    sem.at[len(copies)],
                )
            )
    for copy in copies:
        copy.start()
    for kind in (1, 2):
        for j in range(2):
            picks[kind - 1, j] = ranked(theirs, kind, j)[1]
    for copy in copies:
        copy.wait()


def full_slot(sizes, n, src, left_dims, right_dims, m, r, l):
    blk = sizes[3]
    col = lax.broadcasted_iota(jnp.int32, (1, blk), 1)
    col_live = (col < right_dims[src]).astype(F32).astype(BF16)
    part = lax.dot_general(m * col_live, r, (((1,), (1,)), ((), ())), preferred_element_type=F32)
    row = lax.broadcasted_iota(jnp.int32, (blk, 1), 0)
    part = jnp.where(row < left_dims[src], part, 0.0).astype(BF16)
    return lax.dot_general(l, part, (((1,), (0,)), ((), ())), preferred_element_type=F32)


def start_env(me, k, t, sizes, left, right, right_far, r_dst, l_dst, r_sem, l_sem):
    half_rows = sizes[2]
    o, h = me[1], me[2]
    at_mine = pl.multiple_of((h ^ o) * half_rows, half_rows)
    at_far = pl.multiple_of((1 - (h ^ o)) * half_rows, half_rows)
    pltpu.make_async_copy(right.at[k, t], r_dst.at[pl.ds(at_mine, half_rows)], r_sem).start()
    pltpu.make_async_copy(right_far.at[k, t], r_dst.at[pl.ds(at_far, half_rows)], r_sem).start()
    if l_dst is not None:
        pltpu.make_async_copy(left.at[k, t], l_dst, l_sem).start()


def start_pieces(me, sizes, local, rank, pieces, m_dst, m_sem):
    half_rows = sizes[2]
    quarter = half_rows // 2
    o, h = me[1], me[2]
    for piece, (half, at) in zip(pieces, ((h, o), (h, 1 - o), (1 - h, o), (1 - h, 1 - o))):
        first = pl.multiple_of(half * half_rows + at * quarter, quarter)
        index = local if piece.shape[0] == sizes[1] else rank
        pltpu.make_async_copy(piece.at[index], m_dst.at[pl.ds(first, quarter)], m_sem).start()


def early_kernel(sizes, me, source, left_dims, right_dims, *refs):
    pairs, secs, half_rows, blk = sizes
    own, own_far = refs[0:2]
    near = refs[2:6]
    left, right, right_far = refs[6:9]
    acc, m_buf, r_buf, l_buf, m_sem, r_sem, l_sem = refs[9:]
    o, h = me[1], me[2]
    slots = kinds_of(source, me, pairs, secs, o)
    rank = jnp.int32(0)
    for n, (kind, local, src) in enumerate(slots):
        @pl.when(kind == 0)
        def _():
            mine = pl.multiple_of(h * half_rows, half_rows)
            far = pl.multiple_of((1 - h) * half_rows, half_rows)
            pltpu.make_async_copy(own.at[local], m_buf.at[n, pl.ds(mine, half_rows)], m_sem.at[n]).start()
            pltpu.make_async_copy(own_far.at[local], m_buf.at[n, pl.ds(far, half_rows)], m_sem.at[n]).start()

        @pl.when(kind == 1)
        def _(rank=rank):
            start_pieces(me, sizes, local, rank, near, m_buf.at[n], m_sem.at[n])

        @pl.when(kind <= 1)
        def _():
            start_env(
                me, n // secs, n % secs, sizes, left, right, right_far,
                r_buf.at[n], l_buf.at[n], r_sem.at[n], l_sem.at[n],
            )

        rank = rank + (kind == 1).astype(jnp.int32)

    acc[...] = jnp.zeros_like(acc)
    for n, (kind, local, src) in enumerate(slots):
        @pl.when(kind <= 1)
        def _():
            pltpu.make_async_copy(m_buf.at[n], m_buf.at[n], m_sem.at[n]).wait()
            pltpu.make_async_copy(r_buf.at[n], r_buf.at[n], r_sem.at[n]).wait()
            pltpu.make_async_copy(l_buf.at[n], l_buf.at[n], l_sem.at[n]).wait()
            acc[n % secs] += full_slot(sizes, n, src, left_dims, right_dims, m_buf[n], r_buf[n], l_buf[n])


def late_kernel(sizes, me, source, left_dims, right_dims, *refs):
    pairs, secs, half_rows, blk = sizes
    quarter = half_rows // 2
    mid = refs[0:4]
    late_end, late_end_far, late_mid, late_mid_far = refs[4:8]
    left, right, right_far, left_x, right_x, right_x_far, early = refs[8:15]
    send, keep = refs[15:17]
    acc, m_buf, r_buf, l_buf, lm_buf, lr_buf, ll_buf = refs[17:24]
    m_sem, r_sem, l_sem, lm_sem, lr_sem, ll_sem, acc_sem = refs[24:]
    z, o, h = me[0], me[1], me[2]
    is_end = (z == 0) | (z == 3)
    mine = kinds_of(source, me, pairs, secs, o)
    theirs = kinds_of(source, me, pairs, secs, 1 - o)
    pltpu.make_async_copy(early, acc, acc_sem).start()

    a_slots = [ranked(mine, 2, j) for j in range(2)]
    for j, (n, local, src) in enumerate(a_slots):
        @pl.when(n >= 0)
        def _():
            start_env(
                me, n // secs, n % secs, sizes, left, right, right_far,
                r_buf.at[j], l_buf.at[j], r_sem.at[j], l_sem.at[j],
            )
            start_pieces(me, sizes, local, j, mid, m_buf.at[j], m_sem.at[j])

    late_slots = [ranked(mine, 3, j) for j in range(2)] + [ranked(theirs, 3, j) for j in range(2)]
    for i, (n, local, src) in enumerate(late_slots):
        j = i % 2

        @pl.when(n >= 0)
        def _():
            if i < 2:
                k, t = n // secs, n % secs
                start_env(
                    me, k, t, sizes, left, right, right_far, lr_buf.at[i], None, lr_sem.at[i], None
                )
                for part in range(2):
                    first = pl.multiple_of(part * half_rows + o * quarter, quarter)
                    pltpu.make_async_copy(
                        left.at[k, t, :, pl.ds(first, quarter)],
                        ll_buf.at[i, :, pl.ds(part * quarter, quarter)],
                        ll_sem.at[i],
                    ).start()
            else:
                at_mine = pl.multiple_of((h ^ o) * half_rows, half_rows)
                at_far = pl.multiple_of((1 - (h ^ o)) * half_rows, half_rows)
                pltpu.make_async_copy(right_x.at[j], lr_buf.at[i, pl.ds(at_mine, half_rows)], lr_sem.at[i]).start()
                pltpu.make_async_copy(right_x_far.at[j], lr_buf.at[i, pl.ds(at_far, half_rows)], lr_sem.at[i]).start()
                pltpu.make_async_copy(left_x.at[j], ll_buf.at[i], ll_sem.at[i]).start()
            row_mine = pl.multiple_of(h * quarter, quarter)
            row_far = pl.multiple_of((1 - h) * quarter, quarter)

            @pl.when(is_end)
            def _():
                pltpu.make_async_copy(late_end.at[local], lm_buf.at[i, pl.ds(row_mine, quarter)], lm_sem.at[i]).start()
                pltpu.make_async_copy(late_end_far.at[local], lm_buf.at[i, pl.ds(row_far, quarter)], lm_sem.at[i]).start()

            @pl.when(jnp.logical_not(is_end))
            def _():
                pltpu.make_async_copy(late_mid.at[local], lm_buf.at[i, pl.ds(row_mine, quarter)], lm_sem.at[i]).start()
                pltpu.make_async_copy(late_mid_far.at[local], lm_buf.at[i, pl.ds(row_far, quarter)], lm_sem.at[i]).start()

    pltpu.make_async_copy(early, acc, acc_sem).wait()
    for j, (n, local, src) in enumerate(a_slots):
        @pl.when(n >= 0)
        def _():
            pltpu.make_async_copy(m_buf.at[j], m_buf.at[j], m_sem.at[j]).wait()
            pltpu.make_async_copy(r_buf.at[j], r_buf.at[j], r_sem.at[j]).wait()
            pltpu.make_async_copy(l_buf.at[j], l_buf.at[j], l_sem.at[j]).wait()
            acc[n % secs] += full_slot(sizes, n, src, left_dims, right_dims, m_buf[j], r_buf[j], l_buf[j])

    for i, (n, local, src) in enumerate(late_slots):
        @pl.when(n >= 0)
        def _():
            pltpu.make_async_copy(lm_buf.at[i], lm_buf.at[i], lm_sem.at[i]).wait()
            pltpu.make_async_copy(lr_buf.at[i], lr_buf.at[i], lr_sem.at[i]).wait()
            pltpu.make_async_copy(ll_buf.at[i], ll_buf.at[i], ll_sem.at[i]).wait()
            col = lax.broadcasted_iota(jnp.int32, (1, blk), 1)
            col_live = (col < right_dims[src]).astype(F32).astype(BF16)
            part = lax.dot_general(
                lm_buf[i] * col_live, lr_buf[i], (((1,), (1,)), ((), ())), preferred_element_type=F32
            )
            at = lax.broadcasted_iota(jnp.int32, (half_rows, 1), 0)
            row = at + o * quarter + jnp.where(at < quarter, 0, quarter)
            part = jnp.where(row < left_dims[src], part, 0.0).astype(BF16)
            acc[n % secs] += lax.dot_general(
                ll_buf[i], part, (((1,), (0,)), ((), ())), preferred_element_type=F32
            )

    keep[...] = acc[:, :, : blk // 2]
    send[...] = acc[:, :, blk // 2 :].astype(BF16)


def swap(x, axis):
    return lax.ppermute(x, axis, [(0, 1), (1, 0)])


def swap_on(x, axis, sectors):
    return lax.ppermute(x, ("sector", axis), [(2 * s + i, 2 * s + 1 - i) for s in sectors for i in range(2)])


def four_by_two(wavefunction, left_env, right_env, source, left_dims, right_dims):
    secs, half_rows, blk = wavefunction.shape
    pairs = left_env.shape[0]
    quarter = half_rows // 2
    sizes = (pairs, secs, half_rows, blk)
    z, o, h = lax.axis_index("sector"), lax.axis_index("op"), lax.axis_index("half")
    me = jnp.stack([z, o, h]).astype(jnp.int32)
    smem = pl.BlockSpec(memory_space=pltpu.SMEM)
    any_spec = pl.BlockSpec(memory_space=pl.ANY)
    vmem = pl.BlockSpec(memory_space=pltpu.VMEM)
    needed = pairs * secs

    share = lax.dynamic_slice_in_dim(wavefunction, o * quarter, quarter, axis=1)
    near = lax.ppermute(share, "sector", [(i, i ^ 1) for i in range(4)])
    mid = lax.ppermute(share, "sector", [(i, i ^ 2) for i in range(4)])
    late_mid = lax.ppermute(share, "sector", [(1, 2), (2, 1)])
    late_end = lax.ppermute(mid, "sector", [(1, 0), (2, 3)])

    left_out, right_out, picks = pl.pallas_call(
        functools.partial(plan_kernel, sizes),
        out_shape=(
            jax.ShapeDtypeStruct((2, half_rows, blk // 2), BF16),
            jax.ShapeDtypeStruct((2, half_rows, blk), BF16),
            jax.ShapeDtypeStruct((2, 2), jnp.int32),
        ),
        in_specs=[smem, smem, any_spec, any_spec],
        out_specs=(any_spec, any_spec, smem),
        scratch_shapes=[pltpu.SemaphoreType.DMA((6,))],
        name="plan",
    )(me, source, left_env, right_env)
    right_x = swap(right_out, "op")
    left_x = swap(left_out, "op")
    own_far = swap(wavefunction, "half")
    right_far = swap(right_env, "half")
    right_x_far = swap(right_x, "half")

    def pick(slab, row):
        return jnp.stack([lax.dynamic_index_in_dim(slab, picks[row, j], 0, keepdims=False) for j in range(2)])

    near_x = swap(pick(near, 0), "op")
    mid_x = swap(pick(mid, 1), "op")
    near_refs = (near, near_x, swap(near, "half"), swap(near_x, "half"))
    mid_refs = (mid, mid_x, swap(mid, "half"), swap(mid_x, "half"))
    late_refs = (late_end, swap_on(late_end, "half", (0, 3)), late_mid, swap_on(late_mid, "half", (1, 2)))

    early = pl.pallas_call(
        functools.partial(early_kernel, sizes),
        out_shape=jax.ShapeDtypeStruct((secs, half_rows, blk), F32),
        in_specs=[smem] * 4 + [any_spec] * 9,
        out_specs=vmem,
        scratch_shapes=[
            pltpu.VMEM((needed, blk, blk), BF16),
            pltpu.VMEM((needed, blk, blk), BF16),
            pltpu.VMEM((needed, half_rows, blk), BF16),
        ] + [pltpu.SemaphoreType.DMA((needed,))] * 3,
        compiler_params=pltpu.CompilerParams(vmem_limit_bytes=VMEM_EARLY),
        cost_estimate=pl.CostEstimate(flops=2 * 10**9, bytes_accessed=8 * 10**6, transcendentals=0),
        name="early_slots",
    )(me, source, left_dims, right_dims, wavefunction, own_far, *near_refs, left_env, right_env, right_far)

    send, keep = pl.pallas_call(
        functools.partial(late_kernel, sizes),
        out_shape=(
            jax.ShapeDtypeStruct((secs, half_rows, blk // 2), BF16),
            jax.ShapeDtypeStruct((secs, half_rows, blk // 2), F32),
        ),
        in_specs=[smem] * 4 + [any_spec] * 15,
        out_specs=(vmem, vmem),
        scratch_shapes=[
            pltpu.VMEM((secs, half_rows, blk), F32),
            pltpu.VMEM((2, blk, blk), BF16),
            pltpu.VMEM((2, blk, blk), BF16),
            pltpu.VMEM((2, half_rows, blk), BF16),
            pltpu.VMEM((4, half_rows, blk), BF16),
            pltpu.VMEM((4, blk, blk), BF16),
            pltpu.VMEM((4, half_rows, half_rows), BF16),
        ]
        + [pltpu.SemaphoreType.DMA((2,))] * 3
        + [pltpu.SemaphoreType.DMA((4,))] * 3
        + [pltpu.SemaphoreType.DMA],
        compiler_params=pltpu.CompilerParams(vmem_limit_bytes=VMEM_LATE),
        cost_estimate=pl.CostEstimate(flops=2 * 10**9, bytes_accessed=8 * 10**6, transcendentals=0),
        name="late_slots",
    )(
        me, source, left_dims, right_dims, *mid_refs, *late_refs,
        left_env, right_env, right_far, left_x, right_x, right_x_far, early,
    )
    total = keep + swap(send, "op").astype(F32)
    row_ids = h * half_rows + jnp.arange(half_rows, dtype=jnp.int32)
    col_ids = o * (blk // 2) + jnp.arange(blk // 2, dtype=jnp.int32)
    left_live = lax.dynamic_slice_in_dim(left_dims, z * secs, secs)
    right_live = lax.dynamic_slice_in_dim(right_dims, z * secs, secs)
    live = (row_ids[None, :, None] < left_live[:, None, None]) & (
        col_ids[None, None, :] < right_live[:, None, None]
    )
    return jnp.where(live, total, 0.0).astype(BF16)


def solution(mesh):
    shape = mesh.shape
    fits = (shape["sector"], shape["op"], shape["half"]) == (4, 2, 2)
    return jax.shard_map(
        four_by_two if fits else general,
        mesh=mesh,
        in_specs=(
            P(("group", "sector"), "half", None),
            P("op", ("group", "sector"), "half", None),
            P("op", ("group", "sector"), "half", None),
            P(None, "group"),
            P("group"),
            P("group"),
        ),
        out_specs=P(("group", "sector"), "half", "op"),
        check_vma=False,
    )
```

```python
import functools

import jax
import jax.numpy as jnp
from jax import lax
from jax.experimental import pallas as pl
from jax.experimental.pallas import tpu as pltpu
from jax.sharding import PartitionSpec as P

BF16 = jnp.bfloat16
F32 = jnp.float32
VMEM_LIMIT = 16 * 1024 * 1024


def general(wavefunction, left_env, right_env, source, left_dims, right_dims):
    sec_local, half_rows, blk_cols = wavefunction.shape
    pair_local = left_env.shape[0]
    needed = pair_local * sec_local
    sector_count = lax.axis_size("sector")
    sector_me = lax.axis_index("sector")
    op_me = lax.axis_index("op")
    half_me = lax.axis_index("half")
    places = sector_me * sec_local + jnp.arange(sec_local, dtype=jnp.int32)
    row_ids = half_me * half_rows + jnp.arange(half_rows, dtype=jnp.int32)
    col_ids = jnp.arange(blk_cols, dtype=jnp.int32)
    left_live = jnp.take(left_dims, places)
    right_live = jnp.take(right_dims, places)
    live_mask = (row_ids[None, :, None] < left_live[:, None, None]) & (
        col_ids[None, None, :] < right_live[:, None, None]
    )
    masked = jnp.where(live_mask, wavefunction, jnp.zeros((), wavefunction.dtype))
    wanted = lax.dynamic_slice(source, (op_me * pair_local, 0), (pair_local, source.shape[1]))
    wanted = (
        wanted.reshape(pair_local, sector_count, sec_local)
        .transpose(1, 0, 2)
        .reshape(sector_count, needed)
    )
    own_needs = lax.dynamic_index_in_dim(wanted, sector_me, 0, keepdims=False)
    capacity = -(-needed // sector_count)
    holders = wanted // sec_local
    is_mine = (holders == sector_me).astype(jnp.int32)
    earlier_hits = jnp.cumsum(is_mine, axis=1) - is_mine
    slot_ids = jnp.arange(capacity, dtype=jnp.int32)
    pick_mask = (is_mine[:, :, None] == 1) & (earlier_hits[:, :, None] == slot_ids[None, None, :])
    local_slot = jnp.sum(jnp.where(pick_mask, (wanted % sec_local)[:, :, None], 0), axis=1)
    outgoing = jnp.take(masked, local_slot.reshape(-1), axis=0).reshape(
        sector_count, capacity, half_rows, blk_cols
    )
    incoming = lax.all_to_all(outgoing, "sector", split_axis=0, concat_axis=0, tiled=True)
    owners = own_needs // sec_local
    same_owner = owners[:, None] == owners[None, :]
    order_ids = jnp.arange(needed, dtype=jnp.int32)
    earlier = order_ids[None, :] < order_ids[:, None]
    rank_of = jnp.sum((same_owner & earlier).astype(jnp.int32), axis=1)
    fetched = jnp.take(
        incoming.reshape(sector_count * capacity, half_rows, blk_cols),
        owners * capacity + rank_of,
        axis=0,
    )
    right_rows = right_env.reshape(needed, right_env.shape[2], blk_cols)
    right_part = jnp.einsum(
        "nab,ncb->nac",
        lax.all_gather(fetched, "half", axis=1, tiled=True),
        right_rows,
        preferred_element_type=F32,
    ).astype(BF16)
    right_part = right_part.reshape(pair_local, sec_local, right_part.shape[1], right_part.shape[2])
    partial_sum = jnp.einsum(
        "ksrc,kscj->srj",
        left_env,
        lax.all_gather(right_part, "half", axis=3, tiled=True),
        preferred_element_type=F32,
    )
    summed = lax.psum_scatter(partial_sum, "op", scatter_dimension=2, tiled=True)
    col_width = summed.shape[2]
    out_cols = op_me * col_width + jnp.arange(col_width, dtype=jnp.int32)
    out_mask = (row_ids[None, :, None] < left_live[:, None, None]) & (
        out_cols[None, None, :] < right_live[:, None, None]
    )
    return jnp.where(out_mask, summed, jnp.zeros((), F32)).astype(BF16)


def place():
    return lax.axis_index("sector"), lax.axis_index("op"), lax.axis_index("half")


def slots_of(sizes, source, z, op):
    pairs, secs = sizes[:2]
    found = []
    for n in range(pairs * secs):
        src = source[op * pairs + n // secs, z * secs + n % secs]
        holder = src // secs
        found.append((holder ^ z, src - holder * secs, src))
    return found


def ranked(slots, kind, rank):
    slot, local, source = jnp.int32(-1), jnp.int32(0), jnp.int32(0)
    seen = jnp.int32(0)
    for n, (k, b, s) in enumerate(slots):
        hit = (k == kind) & (seen == rank)
        slot = jnp.where(hit, n, slot)
        local = jnp.where(hit, b, local)
        source = jnp.where(hit, s, source)
        seen = seen + (k == kind).astype(jnp.int32)
    return slot, local, source


def split_kernel(sizes, source, own, share, near_out):
    half_rows = sizes[2]
    quarter = half_rows // 2
    z, o, _ = place()
    share[...] = own[:, pl.ds(pl.multiple_of(o * quarter, quarter), quarter)]
    theirs = slots_of(sizes, source, z ^ 1, o)
    for j in range(2):
        near_out[j] = own[ranked(theirs, 1, j)[1]]


def lend_kernel(sizes, source, left, right, left_out, right_out):
    pairs, secs, half_rows, blk = sizes
    quarter = half_rows // 2
    z, o, _ = place()
    mine = slots_of(sizes, source, z, o)
    for j in range(2):
        n = jnp.maximum(ranked(mine, 3, j)[0], 0)
        k, t = n // secs, n % secs
        right_out[j] = right[k, t]
        for part in range(2):
            first = pl.multiple_of(part * half_rows + (1 - o) * quarter, quarter)
            left_out[j, :, part * quarter : (part + 1) * quarter] = left[k, t, :, pl.ds(first, quarter)]


def pick_kernel(sizes, source, mid, picked):
    z, o, _ = place()
    theirs = slots_of(sizes, source, z, 1 - o)
    for j in range(2):
        picked[j] = mid[ranked(theirs, 2, j)[1]]


def live_columns(sizes, right_dims, src):
    col = lax.broadcasted_iota(jnp.int32, (1, sizes[3]), 1)
    return (col < right_dims[src]).astype(F32).astype(BF16)


def times_right(sizes, m, rights, row, left_live, out):
    half_rows = sizes[2]
    for c, r in enumerate(rights):
        part = lax.dot_general(m, r, (((1,), (1,)), ((), ())), preferred_element_type=F32)
        out[:, c * half_rows : (c + 1) * half_rows] = jnp.where(row < left_live, part, 0.0).astype(BF16)


def early_kernel(sizes, source, left_dims, right_dims, own, own_far, near, near_far, left, right, right_far, acc, m_buf, rp_buf):
    pairs, secs, half_rows, blk = sizes
    z, o, h = place()
    slots = slots_of(sizes, source, z, o)
    mine = pl.ds(pl.multiple_of(h * half_rows, half_rows), half_rows)
    far = pl.ds(pl.multiple_of((1 - h) * half_rows, half_rows), half_rows)
    acc[...] = jnp.zeros_like(acc)
    rank = jnp.int32(0)
    for n, (kind, local, src) in enumerate(slots):
        k, t = n // secs, n % secs
        live = live_columns(sizes, right_dims, src)

        @pl.when(kind == 0)
        def _():
            m_buf[mine] = own[local] * live
            m_buf[far] = own_far[local] * live

        @pl.when(kind == 1)
        def _(rank=rank):
            m_buf[mine] = near[rank] * live
            m_buf[far] = near_far[rank] * live

        @pl.when(kind <= 1)
        def _():
            row = lax.broadcasted_iota(jnp.int32, (blk, 1), 0)
            times_right(sizes, m_buf[...], (right[k, t], right_far[k, t]), row, left_dims[src], rp_buf)
            acc[t] += jnp.dot(left[k, t], rp_buf[...], preferred_element_type=F32)

        rank = rank + (kind == 1).astype(jnp.int32)


def late_kernel(
    sizes, source, left_dims, right_dims, mid, mid_x, mid_far, mid_x_far, end, end_far, inner, inner_far,
    left, right, right_far, left_x, right_x, right_x_far, early, total, send, keep, m_buf, rp_buf,
):
    pairs, secs, half_rows, blk = sizes
    quarter = half_rows // 2
    z, o, h = place()
    is_end = (z == 0) | (z == 3)
    mine = slots_of(sizes, source, z, o)
    theirs = slots_of(sizes, source, z, 1 - o)

    def rows(first):
        return pl.ds(pl.multiple_of(first, quarter), quarter)

    for j in range(2):
        n, local, src = ranked(mine, 2, j)

        @pl.when(n >= 0)
        def _():
            k, t = n // secs, n % secs
            live = live_columns(sizes, right_dims, src)
            m_buf[rows(h * half_rows + o * quarter)] = mid[local] * live
            m_buf[rows(h * half_rows + (1 - o) * quarter)] = mid_x[j] * live
            m_buf[rows((1 - h) * half_rows + o * quarter)] = mid_far[local] * live
            m_buf[rows((1 - h) * half_rows + (1 - o) * quarter)] = mid_x_far[j] * live
            row = lax.broadcasted_iota(jnp.int32, (blk, 1), 0)
            times_right(sizes, m_buf[...], (right[k, t], right_far[k, t]), row, left_dims[src], rp_buf)
            total[t] += jnp.dot(left[k, t], rp_buf[...], preferred_element_type=F32)

    at = lax.broadcasted_iota(jnp.int32, (half_rows, 1), 0)
    row = at + o * quarter + jnp.where(at < quarter, 0, quarter)
    for i in range(4):
        j = i % 2
        n, local, src = ranked(mine if i < 2 else theirs, 3, j)

        @pl.when(n >= 0)
        def _():
            k, t = n // secs, n % secs
            live = live_columns(sizes, right_dims, src)

            @pl.when(is_end)
            def _():
                m_buf[rows(h * quarter)] = end[local] * live
                m_buf[rows((1 - h) * quarter)] = end_far[local] * live

            @pl.when(jnp.logical_not(is_end))
            def _():
                m_buf[rows(h * quarter)] = inner[local] * live
                m_buf[rows((1 - h) * quarter)] = inner_far[local] * live

            if i < 2:
                rights = (right[k, t], right_far[k, t])
                l = jnp.concatenate([left[k, t, :, rows(p * half_rows + o * quarter)] for p in range(2)], axis=1)
            else:
                rights = (right_x[j], right_x_far[j])
                l = left_x[j]
            times_right(sizes, m_buf[:half_rows], rights, row, left_dims[src], rp_buf.at[:half_rows])
            total[t] += jnp.dot(l, rp_buf[:half_rows], preferred_element_type=F32)

    first = pl.multiple_of((h ^ o) * half_rows, half_rows)
    other = pl.multiple_of((1 - (h ^ o)) * half_rows, half_rows)
    keep[...] = total[:, :, pl.ds(first, half_rows)]
    send[...] = total[:, :, pl.ds(other, half_rows)].astype(BF16)


def join_kernel(sizes, left_dims, right_dims, keep, received, out):
    secs, half_rows, blk = sizes[1:]
    z, o, h = place()
    row = h * half_rows + lax.broadcasted_iota(jnp.int32, (half_rows, 1), 0)
    col = o * half_rows + lax.broadcasted_iota(jnp.int32, (1, half_rows), 1)
    for t in range(secs):
        live = (row < left_dims[z * secs + t]) & (col < right_dims[z * secs + t])
        out[t] = jnp.where(live, keep[t] + received[t].astype(F32), 0.0).astype(BF16)


def swap(x, axis):
    return lax.ppermute(x, axis, [(0, 1), (1, 0)])


def swap_on(x, axis, sectors):
    return lax.ppermute(x, ("sector", axis), [(2 * s + i, 2 * s + 1 - i) for s in sectors for i in range(2)])


def four_by_two(wavefunction, left_env, right_env, source, left_dims, right_dims):
    secs, half_rows, blk = wavefunction.shape
    pairs = left_env.shape[0]
    quarter = half_rows // 2
    sizes = (pairs, secs, half_rows, blk)

    def call(kernel, outs, scalars, arrays, scratch=(), flops=0, **options):
        shapes = [jax.ShapeDtypeStruct(shape, dtype) for shape, dtype in outs]
        nbytes = sum(s.size * s.dtype.itemsize for s in [*shapes, *arrays])
        return pl.pallas_call(
            functools.partial(kernel, sizes),
            out_shape=shapes,
            in_specs=[pl.BlockSpec(memory_space=pltpu.SMEM)] * len(scalars)
            + [pl.BlockSpec(memory_space=pltpu.VMEM)] * len(arrays),
            out_specs=[pl.BlockSpec(memory_space=pltpu.VMEM)] * len(shapes),
            scratch_shapes=scratch,
            compiler_params=pltpu.CompilerParams(vmem_limit_bytes=VMEM_LIMIT),
            cost_estimate=pl.CostEstimate(flops=flops, bytes_accessed=nbytes, transcendentals=0),
            name=kernel.__name__,
            **options,
        )(*scalars, *arrays)

    dims = (source, left_dims, right_dims)
    share, near_out = call(
        split_kernel,
        [((secs, quarter, blk), BF16), ((2, half_rows, blk), BF16)],
        (source,),
        (wavefunction,),
    )
    mid = lax.ppermute(share, "sector", [(i, i ^ 2) for i in range(4)])
    near = lax.ppermute(near_out, "sector", [(i, i ^ 1) for i in range(4)])
    left_out, right_out = call(
        lend_kernel,
        [((2, half_rows, half_rows), BF16), ((2, half_rows, blk), BF16)],
        (source,),
        (left_env, right_env),
    )
    right_x = swap(right_out, "op")
    left_x = swap(left_out, "op")
    inner = lax.ppermute(share, "sector", [(1, 2), (2, 1)])
    end = lax.ppermute(mid, "sector", [(1, 0), (2, 3)])
    own_far = swap(wavefunction, "half")
    right_far = swap(right_env, "half")
    near_far = swap(near, "half")
    (picked,) = call(pick_kernel, [((2, quarter, blk), BF16)], (source,), (mid,))
    mid_x = swap(picked, "op")
    buffers = [pltpu.VMEM((blk, blk), BF16), pltpu.VMEM((blk, blk), BF16)]
    (early,) = call(
        early_kernel,
        [((secs, half_rows, blk), F32)],
        dims,
        (wavefunction, own_far, near, near_far, left_env, right_env, right_far),
        buffers,
        flops=4 * 3 * half_rows * blk * blk * 2,
    )
    arrays = (
        mid, mid_x, swap(mid, "half"), swap(mid_x, "half"),
        end, swap_on(end, "half", (0, 3)), inner, swap_on(inner, "half", (1, 2)),
        left_env, right_env, right_far, left_x, right_x, swap(right_x, "half"), early,
    )
    _, send, keep = call(
        late_kernel,
        [
            ((secs, half_rows, blk), F32),
            ((secs, half_rows, half_rows), BF16),
            ((secs, half_rows, half_rows), F32),
        ],
        dims,
        arrays,
        buffers,
        flops=4 * 3 * half_rows * blk * blk * 2,
        input_output_aliases={len(dims) + len(arrays) - 1: 0},
    )
    (out,) = call(
        join_kernel,
        [((secs, half_rows, half_rows), BF16)],
        (left_dims, right_dims),
        (keep, swap(send, "op")),
    )
    return out


def solution(mesh):
    shape = mesh.shape
    fits = (shape["sector"], shape["op"], shape["half"]) == (4, 2, 2)
    return jax.shard_map(
        four_by_two if fits else general,
        mesh=mesh,
        in_specs=(
            P(("group", "sector"), "half", None),
            P("op", ("group", "sector"), "half", None),
            P("op", ("group", "sector"), "half", None),
            P(None, "group"),
            P("group"),
            P("group"),
        ),
        out_specs=P(("group", "sector"), "half", "op"),
        check_vma=False,
    )
```

```python
import functools

import jax
import jax.numpy as jnp
from jax import lax
from jax.experimental import pallas as pl
from jax.experimental.pallas import tpu as pltpu
from jax.sharding import PartitionSpec as P

BF16 = jnp.bfloat16
F32 = jnp.float32
FILL = 30 * 10**9
VMEM_MOST = 61 * 1024 * 1024
VMEM_MUCH = 48 * 1024 * 1024
VMEM_LIMIT = 16 * 1024 * 1024


def general(wavefunction, left_env, right_env, source, left_dims, right_dims):
    sec_local, half_rows, blk_cols = wavefunction.shape
    pair_local = left_env.shape[0]
    needed = pair_local * sec_local
    sector_count = lax.axis_size("sector")
    sector_me = lax.axis_index("sector")
    op_me = lax.axis_index("op")
    half_me = lax.axis_index("half")
    places = sector_me * sec_local + jnp.arange(sec_local, dtype=jnp.int32)
    row_ids = half_me * half_rows + jnp.arange(half_rows, dtype=jnp.int32)
    col_ids = jnp.arange(blk_cols, dtype=jnp.int32)
    left_live = jnp.take(left_dims, places)
    right_live = jnp.take(right_dims, places)
    live_mask = (row_ids[None, :, None] < left_live[:, None, None]) & (
        col_ids[None, None, :] < right_live[:, None, None]
    )
    masked = jnp.where(live_mask, wavefunction, jnp.zeros((), wavefunction.dtype))
    wanted = lax.dynamic_slice(source, (op_me * pair_local, 0), (pair_local, source.shape[1]))
    wanted = (
        wanted.reshape(pair_local, sector_count, sec_local)
        .transpose(1, 0, 2)
        .reshape(sector_count, needed)
    )
    own_needs = lax.dynamic_index_in_dim(wanted, sector_me, 0, keepdims=False)
    capacity = -(-needed // sector_count)
    holders = wanted // sec_local
    is_mine = (holders == sector_me).astype(jnp.int32)
    earlier_hits = jnp.cumsum(is_mine, axis=1) - is_mine
    slot_ids = jnp.arange(capacity, dtype=jnp.int32)
    pick_mask = (is_mine[:, :, None] == 1) & (earlier_hits[:, :, None] == slot_ids[None, None, :])
    local_slot = jnp.sum(jnp.where(pick_mask, (wanted % sec_local)[:, :, None], 0), axis=1)
    outgoing = jnp.take(masked, local_slot.reshape(-1), axis=0).reshape(
        sector_count, capacity, half_rows, blk_cols
    )
    incoming = lax.all_to_all(outgoing, "sector", split_axis=0, concat_axis=0, tiled=True)
    owners = own_needs // sec_local
    same_owner = owners[:, None] == owners[None, :]
    order_ids = jnp.arange(needed, dtype=jnp.int32)
    earlier = order_ids[None, :] < order_ids[:, None]
    rank_of = jnp.sum((same_owner & earlier).astype(jnp.int32), axis=1)
    fetched = jnp.take(
        incoming.reshape(sector_count * capacity, half_rows, blk_cols),
        owners * capacity + rank_of,
        axis=0,
    )
    right_rows = right_env.reshape(needed, right_env.shape[2], blk_cols)
    right_part = jnp.einsum(
        "nab,ncb->nac",
        lax.all_gather(fetched, "half", axis=1, tiled=True),
        right_rows,
        preferred_element_type=F32,
    ).astype(BF16)
    right_part = right_part.reshape(pair_local, sec_local, right_part.shape[1], right_part.shape[2])
    partial_sum = jnp.einsum(
        "ksrc,kscj->srj",
        left_env,
        lax.all_gather(right_part, "half", axis=3, tiled=True),
        preferred_element_type=F32,
    )
    summed = lax.psum_scatter(partial_sum, "op", scatter_dimension=2, tiled=True)
    col_width = summed.shape[2]
    out_cols = op_me * col_width + jnp.arange(col_width, dtype=jnp.int32)
    out_mask = (row_ids[None, :, None] < left_live[:, None, None]) & (
        out_cols[None, None, :] < right_live[:, None, None]
    )
    return jnp.where(out_mask, summed, jnp.zeros((), F32)).astype(BF16)


def place():
    return lax.axis_index("sector"), lax.axis_index("op"), lax.axis_index("half")


def slots_of(sizes, source, z, op):
    pairs, secs = sizes[:2]
    found = []
    for n in range(pairs * secs):
        src = source[op * pairs + n // secs, z * secs + n % secs]
        holder = src // secs
        found.append((holder ^ z, src - holder * secs, src))
    return found


def ranked(slots, kind, rank):
    slot, local, source = jnp.int32(-1), jnp.int32(0), jnp.int32(0)
    seen = jnp.int32(0)
    for n, (k, b, s) in enumerate(slots):
        hit = (k == kind) & (seen == rank)
        slot = jnp.where(hit, n, slot)
        local = jnp.where(hit, b, local)
        source = jnp.where(hit, s, source)
        seen = seen + (k == kind).astype(jnp.int32)
    return slot, local, source


def first_kernel(sizes, source, own, left, right, share, near_out, env_out, l_buf, sem):
    pairs, secs, half_rows, blk = sizes
    quarter = half_rows // 2
    z, o, _ = place()
    theirs = slots_of(sizes, source, z ^ 1, o)
    mine = slots_of(sizes, source, z, o)
    moves = [(own.at[:, pl.ds(pl.multiple_of(o * quarter, quarter), quarter)], share)]
    for j in range(2):
        moves.append((own.at[ranked(theirs, 1, j)[1]], near_out.at[j]))
    for j in range(2):
        n = jnp.maximum(ranked(mine, 3, j)[0], 0)
        moves.append((left.at[n // secs, n % secs], l_buf.at[j]))
        moves.append((right.at[n // secs, n % secs], env_out.at[j, :, :blk]))
    copies = [pltpu.make_async_copy(src, dst, sem.at[i]) for i, (src, dst) in enumerate(moves)]
    for copy in copies:
        copy.start()
    for copy in copies:
        copy.wait()
    for part in range(2):
        first = pl.multiple_of(part * half_rows + (1 - o) * quarter, quarter)
        env_out[:, :, blk + part * quarter : blk + (part + 1) * quarter] = l_buf[:, :, pl.ds(first, quarter)]


def load_kernel(sizes, *refs):
    count = len(refs) // 2
    copies = [pltpu.make_async_copy(refs[i], refs[count + i], refs[-1].at[i]) for i in range(count)]
    for copy in copies:
        copy.start()
    for copy in copies:
        copy.wait()


def pick_kernel(sizes, source, mid, picked):
    z, o, _ = place()
    theirs = slots_of(sizes, source, z, 1 - o)
    for j in range(2):
        picked[j] = mid[ranked(theirs, 2, j)[1]]


def live_columns(sizes, right_dims, src):
    col = lax.broadcasted_iota(jnp.int32, (1, sizes[3]), 1)
    return (col < right_dims[src]).astype(F32).astype(BF16)


def times_right(m, r, row, left_live):
    part = lax.dot_general(m, r, (((1,), (1,)), ((), ())), preferred_element_type=F32)
    return jnp.where(row < left_live, part, 0.0).astype(BF16)


def early_kernel(kind, sizes, source, left_dims, right_dims, near, near_far, left, right, right_far, *rest):
    pairs, secs, half_rows, blk = sizes
    acc, m_buf = rest[-2:]
    z, o, h = place()
    slots = slots_of(sizes, source, z, o)
    mine = pl.ds(pl.multiple_of(h * half_rows, half_rows), half_rows)
    far = pl.ds(pl.multiple_of((1 - h) * half_rows, half_rows), half_rows)
    acc[...] = rest[0][...] if kind == 1 else jnp.zeros_like(acc)
    row = lax.broadcasted_iota(jnp.int32, (blk, 1), 0)
    for j in range(2):
        n, local, src = ranked(slots, kind, j)

        @pl.when(n >= 0)
        def _():
            k, t = n // secs, n % secs
            live = live_columns(sizes, right_dims, src)
            at = j if kind == 1 else local
            m_buf[mine] = near[at] * live
            m_buf[far] = near_far[at] * live
            r = jnp.concatenate(
                [jnp.where(h == 0, right[k, t], right_far[k, t]), jnp.where(h == 0, right_far[k, t], right[k, t])],
                axis=0,
            )
            part = times_right(m_buf[...], r, row, left_dims[src])
            acc[t] += jnp.dot(left[k, t], part, preferred_element_type=F32)


def late_kernel(
    kept, sizes, source, left_dims, right_dims, mid, mid_x, mid_far, mid_x_far, far, far_far,
    left, right, right_far, env_x, env_x_far, early, out, total,
):
    pairs, secs, half_rows, blk = sizes
    quarter = half_rows // 2
    z, o, h = place()
    mine = slots_of(sizes, source, z, o)
    theirs = slots_of(sizes, source, z, 1 - o)
    side = o if kept else 1 - o
    total[...] = early[:, :, pl.ds(pl.multiple_of(side * half_rows, half_rows), half_rows)]
    at = lax.broadcasted_iota(jnp.int32, (quarter, 1), 0)

    def product(m_pieces, firsts, left_pieces, r, n, src):
        live = live_columns(sizes, right_dims, src)
        row = jnp.concatenate([at + first for first in firsts], axis=0)
        left_live = jnp.where(n >= 0, left_dims[src], 0)
        part = times_right(jnp.concatenate(m_pieces, axis=0), r * live, row, left_live)
        return jnp.dot(jnp.concatenate(left_pieces, axis=1), part, preferred_element_type=F32)

    def columns(ref, k, t, first):
        return ref[k, t, :, pl.ds(pl.multiple_of(first, quarter), quarter)]

    found = []
    for j in range(2):
        n, local, src = ranked(mine, 2, j)
        k, t = jnp.maximum(n, 0) // secs, jnp.maximum(n, 0) % secs
        firsts = [half * half_rows + op * quarter for half, op in ((h, o), (h, 1 - o), (1 - h, o), (1 - h, 1 - o))]
        pieces = [mid[local], mid_x[j], mid_far[local], mid_x_far[j]]
        lefts = [columns(left, k, t, first) for first in firsts]
        r = jnp.where(side == h, right[k, t], right_far[k, t])
        found.append((t, product(pieces, firsts, lefts, r, n, src)))

    firsts = [h * half_rows + o * quarter, (1 - h) * half_rows + o * quarter]
    for i in range(4):
        j = i % 2
        n, local, src = ranked(mine if i < 2 else theirs, 3, j)
        k, t = jnp.maximum(n, 0) // secs, jnp.maximum(n, 0) % secs
        pieces = [far[local], far_far[local]]
        if i < 2:
            r = jnp.where(side == h, right[k, t], right_far[k, t])
            lefts = [columns(left, k, t, first) for first in firsts]
        else:
            r = jnp.where(side == h, env_x[j, :, :blk], env_x_far[j, :, :blk])
            lefts = [
                env_x[j, :, pl.ds(pl.multiple_of(blk + first, quarter), quarter)]
                for first in (h * quarter, (1 - h) * quarter)
            ]
        found.append((t, product(pieces, firsts, lefts, r, n, src)))

    for t, term in found:
        total[t] += term
    out[...] = total[...].astype(out.dtype)


def join_kernel(sizes, left_dims, right_dims, keep, received, out):
    secs, half_rows, blk = sizes[1:]
    z, o, h = place()
    row = h * half_rows + lax.broadcasted_iota(jnp.int32, (half_rows, 1), 0)
    col = o * half_rows + lax.broadcasted_iota(jnp.int32, (1, half_rows), 1)
    for t in range(secs):
        live = (row < left_dims[z * secs + t]) & (col < right_dims[z * secs + t])
        out[t] = jnp.where(live, keep[t] + received[t].astype(F32), 0.0).astype(BF16)


def swap(x, axis):
    return lax.ppermute(x, axis, [(0, 1), (1, 0)])


def after(x, *earlier):
    return lax.optimization_barrier((x, *earlier))[0]


def exchange(x, kind):
    return lax.ppermute(x, "sector", [(i, i ^ kind) for i in range(4)])


def four_by_two(wavefunction, left_env, right_env, source, left_dims, right_dims):
    secs, half_rows, blk = wavefunction.shape
    pairs = left_env.shape[0]
    quarter = half_rows // 2
    sizes = (pairs, secs, half_rows, blk)

    def call(kernel, name, outs, scalars, arrays, scratch=(), flops=0, space=pltpu.VMEM, limit=VMEM_LIMIT):
        shapes = [jax.ShapeDtypeStruct(shape, dtype) for shape, dtype in outs]
        nbytes = sum(s.size * s.dtype.itemsize for s in [*shapes, *arrays])
        return pl.pallas_call(
            functools.partial(kernel, sizes),
            out_shape=shapes,
            in_specs=[pl.BlockSpec(memory_space=pltpu.SMEM)] * len(scalars)
            + [pl.BlockSpec(memory_space=space)] * len(arrays),
            out_specs=[pl.BlockSpec(memory_space=pltpu.VMEM)] * len(shapes),
            scratch_shapes=scratch,
            compiler_params=pltpu.CompilerParams(vmem_limit_bytes=limit),
            cost_estimate=pl.CostEstimate(flops=flops, bytes_accessed=nbytes, transcendentals=0),
            name=name,
        )(*scalars, *arrays)

    dims = (source, left_dims, right_dims)
    share, near_out, env_out = call(
        first_kernel,
        "first",
        [
            ((secs, quarter, blk), BF16),
            ((2, half_rows, blk), BF16),
            ((2, half_rows, blk + half_rows), BF16),
        ],
        (source,),
        (wavefunction, left_env, right_env),
        [pltpu.VMEM((2, half_rows, blk), BF16), pltpu.SemaphoreType.DMA((7,))],
        space=pltpu.HBM,
        limit=VMEM_MOST,
    )
    mid = exchange(share, 2)
    near = exchange(near_out, 1)
    env_x = swap(env_out, "op")
    own_far = swap(wavefunction, "half")
    right_far = swap(right_env, "half")
    loaded = (after(wavefunction, share), left_env, right_env)
    own, left, right = call(
        load_kernel,
        "load",
        [(x.shape, x.dtype) for x in loaded],
        (),
        loaded,
        [pltpu.SemaphoreType.DMA((3,))],
        flops=FILL,
        space=pltpu.HBM,
        limit=VMEM_MUCH,
    )
    mid, near, env_x, own_far, right_far = (after(x, own) for x in (mid, near, env_x, own_far, right_far))
    far = exchange(mid, 1)
    envs = (left, right, right_far)
    total = [((secs, half_rows, blk), F32)]
    block = [pltpu.VMEM((blk, blk), BF16)]
    (picked,) = call(pick_kernel, "pick", [((2, quarter, blk), BF16)], (source,), (after(mid, env_x),))
    mid_x = swap(picked, "op")
    near_far = swap(near, "half")
    mid_far = swap(mid, "half")
    env_x_far = swap(env_x, "half")
    (early,) = call(functools.partial(early_kernel, 0), "own_slots", total, dims, (own, own_far, *envs), block)
    (early,) = call(
        functools.partial(early_kernel, 1),
        "near_slots",
        total,
        dims,
        (near, after(near_far, mid_far, env_x_far), *envs, early),
        block,
        flops=FILL,
    )
    mid_x, far = after(mid_x, early), after(far, early)
    mid_x_far = swap(mid_x, "half")
    far_far = swap(far, "half")
    arrays = (mid, mid_x, mid_far, mid_x_far, far, far_far, *envs, env_x, env_x_far, early)
    buffers = [pltpu.VMEM((secs, half_rows, half_rows), F32)]
    flops = 2 * 3 * half_rows * blk * blk * 2
    columns = (secs, half_rows, half_rows)
    (send,) = call(
        functools.partial(late_kernel, False), "late_sent", [(columns, BF16)], dims, arrays, buffers, flops
    )
    received = swap(send, "op")
    (keep,) = call(
        functools.partial(late_kernel, True), "late_kept", [(columns, F32)], dims, arrays, buffers, flops
    )
    (out,) = call(join_kernel, "join", [(columns, BF16)], (left_dims, right_dims), (keep, received))
    return out


def solution(mesh):
    shape = mesh.shape
    fits = (shape["sector"], shape["op"], shape["half"]) == (4, 2, 2)
    return jax.shard_map(
        four_by_two if fits else general,
        mesh=mesh,
        in_specs=(
            P(("group", "sector"), "half", None),
            P("op", ("group", "sector"), "half", None),
            P("op", ("group", "sector"), "half", None),
            P(None, "group"),
            P("group"),
            P("group"),
        ),
        out_specs=P(("group", "sector"), "half", "op"),
        check_vma=False,
    )
```

```python
import functools

import jax
import jax.numpy as jnp
from jax import lax
from jax.experimental import pallas as pl
from jax.experimental.pallas import tpu as pltpu
from jax.sharding import PartitionSpec as P

BF16 = jnp.bfloat16
F32 = jnp.float32
FILL = 30 * 10**9
VMEM_MOST = 61 * 1024 * 1024
VMEM_MUCH = 48 * 1024 * 1024
VMEM_LIMIT = 16 * 1024 * 1024


def general(wavefunction, left_env, right_env, source, left_dims, right_dims):
    sec_local, half_rows, blk_cols = wavefunction.shape
    pair_local = left_env.shape[0]
    needed = pair_local * sec_local
    sector_count = lax.axis_size("sector")
    sector_me = lax.axis_index("sector")
    op_me = lax.axis_index("op")
    half_me = lax.axis_index("half")
    places = sector_me * sec_local + jnp.arange(sec_local, dtype=jnp.int32)
    row_ids = half_me * half_rows + jnp.arange(half_rows, dtype=jnp.int32)
    col_ids = jnp.arange(blk_cols, dtype=jnp.int32)
    left_live = jnp.take(left_dims, places)
    right_live = jnp.take(right_dims, places)
    live_mask = (row_ids[None, :, None] < left_live[:, None, None]) & (
        col_ids[None, None, :] < right_live[:, None, None]
    )
    masked = jnp.where(live_mask, wavefunction, jnp.zeros((), wavefunction.dtype))
    wanted = lax.dynamic_slice(source, (op_me * pair_local, 0), (pair_local, source.shape[1]))
    wanted = (
        wanted.reshape(pair_local, sector_count, sec_local)
        .transpose(1, 0, 2)
        .reshape(sector_count, needed)
    )
    own_needs = lax.dynamic_index_in_dim(wanted, sector_me, 0, keepdims=False)
    capacity = -(-needed // sector_count)
    holders = wanted // sec_local
    is_mine = (holders == sector_me).astype(jnp.int32)
    earlier_hits = jnp.cumsum(is_mine, axis=1) - is_mine
    slot_ids = jnp.arange(capacity, dtype=jnp.int32)
    pick_mask = (is_mine[:, :, None] == 1) & (earlier_hits[:, :, None] == slot_ids[None, None, :])
    local_slot = jnp.sum(jnp.where(pick_mask, (wanted % sec_local)[:, :, None], 0), axis=1)
    outgoing = jnp.take(masked, local_slot.reshape(-1), axis=0).reshape(
        sector_count, capacity, half_rows, blk_cols
    )
    incoming = lax.all_to_all(outgoing, "sector", split_axis=0, concat_axis=0, tiled=True)
    owners = own_needs // sec_local
    same_owner = owners[:, None] == owners[None, :]
    order_ids = jnp.arange(needed, dtype=jnp.int32)
    earlier = order_ids[None, :] < order_ids[:, None]
    rank_of = jnp.sum((same_owner & earlier).astype(jnp.int32), axis=1)
    fetched = jnp.take(
        incoming.reshape(sector_count * capacity, half_rows, blk_cols),
        owners * capacity + rank_of,
        axis=0,
    )
    right_rows = right_env.reshape(needed, right_env.shape[2], blk_cols)
    right_part = jnp.einsum(
        "nab,ncb->nac",
        lax.all_gather(fetched, "half", axis=1, tiled=True),
        right_rows,
        preferred_element_type=F32,
    ).astype(BF16)
    right_part = right_part.reshape(pair_local, sec_local, right_part.shape[1], right_part.shape[2])
    partial_sum = jnp.einsum(
        "ksrc,kscj->srj",
        left_env,
        lax.all_gather(right_part, "half", axis=3, tiled=True),
        preferred_element_type=F32,
    )
    summed = lax.psum_scatter(partial_sum, "op", scatter_dimension=2, tiled=True)
    col_width = summed.shape[2]
    out_cols = op_me * col_width + jnp.arange(col_width, dtype=jnp.int32)
    out_mask = (row_ids[None, :, None] < left_live[:, None, None]) & (
        out_cols[None, None, :] < right_live[:, None, None]
    )
    return jnp.where(out_mask, summed, jnp.zeros((), F32)).astype(BF16)


def place():
    return lax.axis_index("sector"), lax.axis_index("op"), lax.axis_index("half")


def slots_of(sizes, source, z, op):
    pairs, secs = sizes[:2]
    found = []
    for n in range(pairs * secs):
        src = source[op * pairs + n // secs, z * secs + n % secs]
        holder = src // secs
        found.append((holder ^ z, src - holder * secs, src))
    return found


def ranked(slots, kind, rank):
    slot, local, source = jnp.int32(-1), jnp.int32(0), jnp.int32(0)
    seen = jnp.int32(0)
    for n, (k, b, s) in enumerate(slots):
        hit = (k == kind) & (seen == rank)
        slot = jnp.where(hit, n, slot)
        local = jnp.where(hit, b, local)
        source = jnp.where(hit, s, source)
        seen = seen + (k == kind).astype(jnp.int32)
    return slot, local, source


def first_kernel(sizes, source_hbm, own, left, right, share, near_out, env_out, source, l_buf, sem):
    pairs, secs, half_rows, blk = sizes
    quarter = half_rows // 2
    z, o, _ = place()
    rows = pl.ds(pl.multiple_of(o * quarter, quarter), quarter)
    copies = [
        pltpu.make_async_copy(source_hbm, source, sem.at[0]),
        pltpu.make_async_copy(own.at[:, rows], share, sem.at[1]),
    ]
    copies[0].start()
    copies[1].start()
    copies[0].wait()
    theirs = slots_of(sizes, source, z ^ 1, o)
    mine = slots_of(sizes, source, z, o)
    moves = [(own.at[ranked(theirs, 1, j)[1]], near_out.at[j]) for j in range(2)]
    for j in range(2):
        n = jnp.maximum(ranked(mine, 3, j)[0], 0)
        moves.append((left.at[n // secs, n % secs], l_buf.at[j]))
        moves.append((right.at[n // secs, n % secs], env_out.at[j, :, :blk]))
    copies = copies[1:] + [pltpu.make_async_copy(src, dst, sem.at[2 + i]) for i, (src, dst) in enumerate(moves)]
    for copy in copies[1:]:
        copy.start()
    for copy in copies:
        copy.wait()
    for part in range(2):
        first = pl.multiple_of(part * half_rows + (1 - o) * quarter, quarter)
        env_out[:, :, blk + part * quarter : blk + (part + 1) * quarter] = l_buf[:, :, pl.ds(first, quarter)]


def load_kernel(sizes, *refs):
    count = len(refs) // 2
    copies = [pltpu.make_async_copy(refs[i], refs[count + i], refs[-1].at[i]) for i in range(count)]
    for copy in copies:
        copy.start()
    for copy in copies:
        copy.wait()


def pick_kernel(sizes, source, mid, picked):
    z, o, _ = place()
    theirs = slots_of(sizes, source, z, 1 - o)
    for j in range(2):
        picked[j] = mid[ranked(theirs, 2, j)[1]]


def live_columns(sizes, right_dims, src):
    col = lax.broadcasted_iota(jnp.int32, (1, sizes[3]), 1)
    return (col < right_dims[src]).astype(F32).astype(BF16)


def times_right(m, r, row, left_live):
    part = lax.dot_general(m, r, (((1,), (1,)), ((), ())), preferred_element_type=F32)
    return jnp.where(row < left_live, part, 0.0).astype(BF16)


def own_kernel(sizes, source, left_dims, right_dims, own, own_far, left, right, right_far, acc, m_buf):
    pairs, secs, half_rows, blk = sizes
    z, o, h = place()
    slots = slots_of(sizes, source, z, o)
    acc[...] = jnp.zeros_like(acc)
    row = lax.broadcasted_iota(jnp.int32, (blk, 1), 0)
    for j in range(2):
        n, local, src = ranked(slots, 0, j)

        @pl.when(n >= 0)
        def _():
            k, t = n // secs, n % secs
            live = live_columns(sizes, right_dims, src)
            for half, ref in ((h, own), (1 - h, own_far)):
                m_buf[pl.ds(pl.multiple_of(half * half_rows, half_rows), half_rows)] = ref[local] * live
            r = jnp.concatenate(
                [jnp.where(h == 0, right[k, t], right_far[k, t]), jnp.where(h == 0, right_far[k, t], right[k, t])],
                axis=0,
            )
            part = times_right(m_buf[...], r, row, left_dims[src])
            acc[t] += jnp.dot(left[k, t], part, preferred_element_type=F32)


def late_kernel(
    kept, sizes, source, left_dims, right_dims, near, near_far, mid, mid_x, mid_far, mid_x_far, far, far_far,
    left, right, right_far, env_x, env_x_far, early, out, total,
):
    pairs, secs, half_rows, blk = sizes
    quarter = half_rows // 2
    z, o, h = place()
    mine = slots_of(sizes, source, z, o)
    theirs = slots_of(sizes, source, z, 1 - o)
    side = o if kept else 1 - o
    total[...] = early[:, :, pl.ds(pl.multiple_of(side * half_rows, half_rows), half_rows)]
    parts = []

    def add(slot, pieces, firsts, env=None):
        n, _, src = slot
        k, t = jnp.maximum(n, 0) // secs, jnp.maximum(n, 0) % secs
        size = pieces[0].shape[0]
        if env is None:
            r = jnp.where(side == h, right[k, t], right_far[k, t])
            lefts = [left[k, t, :, pl.ds(pl.multiple_of(first, size), size)] for first in firsts]
        else:
            r = jnp.where(side == h, env_x[env, :, :blk], env_x_far[env, :, :blk])
            lefts = [env_x[env, :, pl.ds(pl.multiple_of(blk + half * quarter, quarter), quarter)] for half in (h, 1 - h)]
        at = lax.broadcasted_iota(jnp.int32, (size, 1), 0)
        row = jnp.concatenate([at + first for first in firsts], axis=0)
        live = live_columns(sizes, right_dims, src)
        left_live = jnp.where(n >= 0, left_dims[src], 0)
        part = times_right(jnp.concatenate(pieces, axis=0), r * live, row, left_live)
        parts.append((t, jnp.concatenate(lefts, axis=1), part))

    halves = [h * half_rows, (1 - h) * half_rows]
    ops = [o * quarter, (1 - o) * quarter]
    for j in range(2):
        add(ranked(mine, 1, j), [near[j], near_far[j]], halves)
        slot = ranked(mine, 2, j)
        pieces = [mid[slot[1]], mid_x[j], mid_far[slot[1]], mid_x_far[j]]
        add(slot, pieces, [half + op for half in halves for op in ops])
        for slot, env in ((ranked(mine, 3, j), None), (ranked(theirs, 3, j), j)):
            add(slot, [far[slot[1]], far_far[slot[1]]], [half + ops[0] for half in halves], env)
    for t, l, part in parts:
        total[t] += jnp.dot(l, part, preferred_element_type=F32)
    out[...] = total[...].astype(out.dtype)


def join_kernel(sizes, left_dims, right_dims, keep, received, out):
    secs, half_rows, blk = sizes[1:]
    z, o, h = place()
    row = h * half_rows + lax.broadcasted_iota(jnp.int32, (half_rows, 1), 0)
    col = o * half_rows + lax.broadcasted_iota(jnp.int32, (1, half_rows), 1)
    for t in range(secs):
        live = (row < left_dims[z * secs + t]) & (col < right_dims[z * secs + t])
        out[t] = jnp.where(live, keep[t] + received[t].astype(F32), 0.0).astype(BF16)


def swap(x, axis):
    return lax.ppermute(x, axis, [(0, 1), (1, 0)])


def after(x, *earlier):
    return lax.optimization_barrier((x, *earlier))[0]


def exchange(x, kind):
    return lax.ppermute(x, "sector", [(i, i ^ kind) for i in range(4)])


def four_by_two(wavefunction, left_env, right_env, source, left_dims, right_dims):
    secs, half_rows, blk = wavefunction.shape
    pairs = left_env.shape[0]
    quarter = half_rows // 2
    sizes = (pairs, secs, half_rows, blk)

    def call(kernel, name, outs, scalars, arrays, scratch=(), flops=0, space=pltpu.VMEM, limit=VMEM_LIMIT):
        shapes = [jax.ShapeDtypeStruct(shape, dtype) for shape, dtype in outs]
        nbytes = sum(s.size * s.dtype.itemsize for s in [*shapes, *arrays])
        return pl.pallas_call(
            functools.partial(kernel, sizes),
            out_shape=shapes,
            in_specs=[pl.BlockSpec(memory_space=pltpu.SMEM)] * len(scalars)
            + [pl.BlockSpec(memory_space=space)] * len(arrays),
            out_specs=[pl.BlockSpec(memory_space=pltpu.VMEM)] * len(shapes),
            scratch_shapes=scratch,
            compiler_params=pltpu.CompilerParams(vmem_limit_bytes=limit),
            cost_estimate=pl.CostEstimate(flops=flops, bytes_accessed=nbytes, transcendentals=0),
            name=name,
        )(*scalars, *arrays)

    dims = (source, left_dims, right_dims)
    share, near_out, env_out = call(
        first_kernel,
        "first",
        [((secs, quarter, blk), BF16), ((2, half_rows, blk), BF16), ((2, half_rows, blk + half_rows), BF16)],
        (),
        (source, wavefunction, left_env, right_env),
        [
            pltpu.SMEM(source.shape, source.dtype),
            pltpu.VMEM((2, half_rows, blk), BF16),
            pltpu.SemaphoreType.DMA((8,)),
        ],
        space=pltpu.HBM,
        limit=VMEM_MOST,
    )
    mid = exchange(share, 2)
    near = exchange(near_out, 1)
    env_x = swap(env_out, "op")
    own_far = swap(wavefunction, "half")
    right_far = swap(right_env, "half")
    loaded = (after(wavefunction, env_out), left_env, right_env)
    own, left, right = call(
        load_kernel,
        "load",
        [(x.shape, x.dtype) for x in loaded],
        (),
        loaded,
        [pltpu.SemaphoreType.DMA((3,))],
        flops=FILL,
        space=pltpu.HBM,
        limit=VMEM_MUCH,
    )
    mid, near, env_x, own_far, right_far = (after(x, own) for x in (mid, near, env_x, own_far, right_far))
    envs = (left, right, right_far)

    far = exchange(mid, 1)
    (picked,) = call(pick_kernel, "pick", [((2, quarter, blk), BF16)], (source,), (mid,))
    mid_x = swap(picked, "op")
    (early,) = call(
        own_kernel,
        "own_slots",
        [((secs, half_rows, blk), F32)],
        dims,
        (own, after(own_far, picked), *envs),
        [pltpu.VMEM((blk, blk), BF16)],
        flops=FILL,
    )
    mid_x, env_x = after(mid_x, early), after(env_x, early)
    mid_x_far = swap(mid_x, "half")
    mid_far = swap(after(mid, mid_x), "half")
    env_x_far = swap(after(env_x, mid_x), "half")
    far = after(far, early, mid_x_far)
    near = after(near, mid_x)
    arrays = (
        near, swap(near, "half"), mid, mid_x, mid_far, mid_x_far, far, swap(far, "half"),
        *envs, env_x, env_x_far, early,
    )
    buffers = [pltpu.VMEM((secs, half_rows, half_rows), F32)]
    flops = 2 * 3 * half_rows * blk * blk * 2
    columns = (secs, half_rows, half_rows)
    (send,) = call(
        functools.partial(late_kernel, False), "late_sent", [(columns, BF16)], dims, arrays, buffers, flops
    )
    received = swap(send, "op")
    (keep,) = call(
        functools.partial(late_kernel, True), "late_kept", [(columns, F32)], dims, arrays, buffers, flops
    )
    (out,) = call(join_kernel, "join", [(columns, BF16)], (left_dims, right_dims), (keep, received))
    return out


def solution(mesh):
    shape = mesh.shape
    fits = (shape["sector"], shape["op"], shape["half"]) == (4, 2, 2)
    return jax.shard_map(
        four_by_two if fits else general,
        mesh=mesh,
        in_specs=(
            P(("group", "sector"), "half", None),
            P("op", ("group", "sector"), "half", None),
            P("op", ("group", "sector"), "half", None),
            P(None, "group"),
            P("group"),
            P("group"),
        ),
        out_specs=P(("group", "sector"), "half", "op"),
        check_vma=False,
    )
```

```python
import functools

import jax
import jax.numpy as jnp
from jax import lax
from jax.experimental import pallas as pl
from jax.experimental.pallas import tpu as pltpu
from jax.sharding import PartitionSpec as P

BF16 = jnp.bfloat16
F32 = jnp.float32
FILL = 30 * 10**9
VMEM_MOST = 61 * 1024 * 1024
VMEM_MUCH = 48 * 1024 * 1024
VMEM_LIMIT = 16 * 1024 * 1024


def general(wavefunction, left_env, right_env, source, left_dims, right_dims):
    sec_local, half_rows, blk_cols = wavefunction.shape
    pair_local = left_env.shape[0]
    needed = pair_local * sec_local
    sector_count = lax.axis_size("sector")
    sector_me = lax.axis_index("sector")
    op_me = lax.axis_index("op")
    half_me = lax.axis_index("half")
    places = sector_me * sec_local + jnp.arange(sec_local, dtype=jnp.int32)
    row_ids = half_me * half_rows + jnp.arange(half_rows, dtype=jnp.int32)
    col_ids = jnp.arange(blk_cols, dtype=jnp.int32)
    left_live = jnp.take(left_dims, places)
    right_live = jnp.take(right_dims, places)
    live_mask = (row_ids[None, :, None] < left_live[:, None, None]) & (
        col_ids[None, None, :] < right_live[:, None, None]
    )
    masked = jnp.where(live_mask, wavefunction, jnp.zeros((), wavefunction.dtype))
    wanted = lax.dynamic_slice(source, (op_me * pair_local, 0), (pair_local, source.shape[1]))
    wanted = (
        wanted.reshape(pair_local, sector_count, sec_local)
        .transpose(1, 0, 2)
        .reshape(sector_count, needed)
    )
    own_needs = lax.dynamic_index_in_dim(wanted, sector_me, 0, keepdims=False)
    capacity = -(-needed // sector_count)
    holders = wanted // sec_local
    is_mine = (holders == sector_me).astype(jnp.int32)
    earlier_hits = jnp.cumsum(is_mine, axis=1) - is_mine
    slot_ids = jnp.arange(capacity, dtype=jnp.int32)
    pick_mask = (is_mine[:, :, None] == 1) & (earlier_hits[:, :, None] == slot_ids[None, None, :])
    local_slot = jnp.sum(jnp.where(pick_mask, (wanted % sec_local)[:, :, None], 0), axis=1)
    outgoing = jnp.take(masked, local_slot.reshape(-1), axis=0).reshape(
        sector_count, capacity, half_rows, blk_cols
    )
    incoming = lax.all_to_all(outgoing, "sector", split_axis=0, concat_axis=0, tiled=True)
    owners = own_needs // sec_local
    same_owner = owners[:, None] == owners[None, :]
    order_ids = jnp.arange(needed, dtype=jnp.int32)
    earlier = order_ids[None, :] < order_ids[:, None]
    rank_of = jnp.sum((same_owner & earlier).astype(jnp.int32), axis=1)
    fetched = jnp.take(
        incoming.reshape(sector_count * capacity, half_rows, blk_cols),
        owners * capacity + rank_of,
        axis=0,
    )
    right_rows = right_env.reshape(needed, right_env.shape[2], blk_cols)
    right_part = jnp.einsum(
        "nab,ncb->nac",
        lax.all_gather(fetched, "half", axis=1, tiled=True),
        right_rows,
        preferred_element_type=F32,
    ).astype(BF16)
    right_part = right_part.reshape(pair_local, sec_local, right_part.shape[1], right_part.shape[2])
    partial_sum = jnp.einsum(
        "ksrc,kscj->srj",
        left_env,
        lax.all_gather(right_part, "half", axis=3, tiled=True),
        preferred_element_type=F32,
    )
    summed = lax.psum_scatter(partial_sum, "op", scatter_dimension=2, tiled=True)
    col_width = summed.shape[2]
    out_cols = op_me * col_width + jnp.arange(col_width, dtype=jnp.int32)
    out_mask = (row_ids[None, :, None] < left_live[:, None, None]) & (
        out_cols[None, None, :] < right_live[:, None, None]
    )
    return jnp.where(out_mask, summed, jnp.zeros((), F32)).astype(BF16)


def place():
    return lax.axis_index("sector"), lax.axis_index("op"), lax.axis_index("half")


def slots_of(sizes, source, z, op):
    pairs, secs = sizes[:2]
    found = []
    for n in range(pairs * secs):
        src = source[op * pairs + n // secs, z * secs + n % secs]
        holder = src // secs
        found.append((holder ^ z, src - holder * secs, src))
    return found


def ranked(slots, kind, rank):
    slot, local, source = jnp.int32(-1), jnp.int32(0), jnp.int32(0)
    seen = jnp.int32(0)
    for n, (k, b, s) in enumerate(slots):
        hit = (k == kind) & (seen == rank)
        slot = jnp.where(hit, n, slot)
        local = jnp.where(hit, b, local)
        source = jnp.where(hit, s, source)
        seen = seen + (k == kind).astype(jnp.int32)
    return slot, local, source


def first_kernel(sizes, source_hbm, own, left, right, share, near_out, env_out, source, own_buf, left_buf, sem):
    pairs, secs, half_rows, blk = sizes
    quarter = half_rows // 2
    z, o, _ = place()
    copies = [pltpu.make_async_copy(source_hbm, source, sem.at[0]), pltpu.make_async_copy(own, own_buf, sem.at[1])]
    for copy in copies:
        copy.start()
    copies[0].wait()
    mine = slots_of(sizes, source, z, o)
    for j in range(2):
        n = jnp.maximum(ranked(mine, 3, j)[0], 0)
        for src, dst in ((right, env_out.at[j]), (left, left_buf.at[j])):
            copy = pltpu.make_async_copy(src.at[n // secs, n % secs], dst, sem.at[len(copies)])
            copy.start()
            copies.append(copy)
    theirs = slots_of(sizes, source, z ^ 1, o)
    copies[1].wait()
    share[...] = own_buf[:, pl.ds(pl.multiple_of(o * quarter, quarter), quarter)]
    for j in range(2):
        near_out[j] = own_buf[ranked(theirs, 1, j)[1]]
    for copy in copies[2:]:
        copy.wait()
    for j in range(2):
        for part in range(2):
            first = pl.multiple_of(part * half_rows + (1 - o) * quarter, quarter)
            to = j * half_rows + part * quarter
            env_out[2, :, to : to + quarter] = left_buf[j, :, pl.ds(first, quarter)]


def load_kernel(sizes, *refs):
    count = len(refs) // 2
    copies = [pltpu.make_async_copy(refs[i], refs[count + i], refs[-1].at[i]) for i in range(count)]
    for copy in copies:
        copy.start()
    for copy in copies:
        copy.wait()


def pick_kernel(sizes, source, mid, picked):
    z, o, _ = place()
    theirs = slots_of(sizes, source, z, 1 - o)
    for j in range(2):
        picked[j] = mid[ranked(theirs, 2, j)[1]]


def live_columns(sizes, right_dims, src):
    col = lax.broadcasted_iota(jnp.int32, (1, sizes[3]), 1)
    return (col < right_dims[src]).astype(F32).astype(BF16)


def times_right(m, r, row, left_live):
    part = lax.dot_general(m, r, (((1,), (1,)), ((), ())), preferred_element_type=F32)
    return jnp.where(row < left_live, part, 0.0).astype(BF16)


def own_kernel(sizes, source, left_dims, right_dims, own, own_far, left, right, right_far, acc, m_buf):
    pairs, secs, half_rows, blk = sizes
    z, o, h = place()
    slots = slots_of(sizes, source, z, o)
    acc[...] = jnp.zeros_like(acc)
    row = lax.broadcasted_iota(jnp.int32, (blk, 1), 0)
    for j in range(2):
        n, local, src = ranked(slots, 0, j)

        @pl.when(n >= 0)
        def _():
            k, t = n // secs, n % secs
            live = live_columns(sizes, right_dims, src)
            for half, ref in ((h, own), (1 - h, own_far)):
                m_buf[pl.ds(pl.multiple_of(half * half_rows, half_rows), half_rows)] = ref[local] * live
            r = jnp.concatenate(
                [jnp.where(h == 0, right[k, t], right_far[k, t]), jnp.where(h == 0, right_far[k, t], right[k, t])],
                axis=0,
            )
            part = times_right(m_buf[...], r, row, left_dims[src])
            acc[t] += jnp.dot(left[k, t], part, preferred_element_type=F32)


def late_kernel(
    kept, sizes, source, left_dims, right_dims, near, near_far, mid, mid_x, mid_far, mid_x_far, far, far_far,
    left, right, right_far, env_x, env_x_far, early, out, total,
):
    pairs, secs, half_rows, blk = sizes
    quarter = half_rows // 2
    z, o, h = place()
    mine = slots_of(sizes, source, z, o)
    theirs = slots_of(sizes, source, z, 1 - o)
    side = o if kept else 1 - o
    total[...] = early[:, :, pl.ds(pl.multiple_of(side * half_rows, half_rows), half_rows)]
    parts = []

    def add(slot, pieces, firsts, env=None):
        n, _, src = slot
        k, t = jnp.maximum(n, 0) // secs, jnp.maximum(n, 0) % secs
        size = pieces[0].shape[0]
        if env is None:
            r = jnp.where(side == h, right[k, t], right_far[k, t])
            lefts = [left[k, t, :, pl.ds(pl.multiple_of(first, size), size)] for first in firsts]
        else:
            r = jnp.where(side == h, env_x[env], env_x_far[env])
            lefts = [
                env_x[2, :, pl.ds(pl.multiple_of(env * half_rows + half * quarter, quarter), quarter)]
                for half in (h, 1 - h)
            ]
        at = lax.broadcasted_iota(jnp.int32, (size, 1), 0)
        row = jnp.concatenate([at + first for first in firsts], axis=0)
        live = live_columns(sizes, right_dims, src)
        left_live = jnp.where(n >= 0, left_dims[src], 0)
        part = times_right(jnp.concatenate(pieces, axis=0), r * live, row, left_live)
        parts.append((t, jnp.concatenate(lefts, axis=1), part))

    halves = [h * half_rows, (1 - h) * half_rows]
    ops = [o * quarter, (1 - o) * quarter]
    for j in range(2):
        add(ranked(mine, 1, j), [near[j], near_far[j]], halves)
        slot = ranked(mine, 2, j)
        pieces = [mid[slot[1]], mid_x[j], mid_far[slot[1]], mid_x_far[j]]
        add(slot, pieces, [half + op for half in halves for op in ops])
        for slot, env in ((ranked(mine, 3, j), None), (ranked(theirs, 3, j), j)):
            add(slot, [far[slot[1]], far_far[slot[1]]], [half + ops[0] for half in halves], env)
    for t, l, part in parts:
        total[t] += jnp.dot(l, part, preferred_element_type=F32)
    out[...] = total[...].astype(out.dtype)


def join_kernel(sizes, left_dims, right_dims, keep, received, out, held, sem):
    secs, half_rows, blk = sizes[1:]
    z, o, h = place()
    row = h * half_rows + lax.broadcasted_iota(jnp.int32, (half_rows, 1), 0)
    col = o * half_rows + lax.broadcasted_iota(jnp.int32, (1, half_rows), 1)
    copies = [pltpu.make_async_copy(held.at[t], out.at[t], sem.at[t]) for t in range(secs)]
    for t in range(secs):
        live = (row < left_dims[z * secs + t]) & (col < right_dims[z * secs + t])
        held[t] = jnp.where(live, keep[t] + received[t].astype(F32), 0.0).astype(BF16)
        copies[t].start()
    for copy in copies:
        copy.wait()


def swap(x, axis):
    return lax.ppermute(x, axis, [(0, 1), (1, 0)])


def after(x, *earlier):
    return lax.optimization_barrier((x, *earlier))[0]


def exchange(x, kind):
    return lax.ppermute(x, "sector", [(i, i ^ kind) for i in range(4)])


def four_by_two(wavefunction, left_env, right_env, source, left_dims, right_dims):
    secs, half_rows, blk = wavefunction.shape
    pairs = left_env.shape[0]
    quarter = half_rows // 2
    sizes = (pairs, secs, half_rows, blk)

    def call(
        kernel, name, outs, scalars, arrays, scratch=(), flops=0, space=pltpu.VMEM, limit=VMEM_LIMIT, to=pltpu.VMEM
    ):
        shapes = [jax.ShapeDtypeStruct(shape, dtype) for shape, dtype in outs]
        nbytes = sum(s.size * s.dtype.itemsize for s in [*shapes, *arrays])
        return pl.pallas_call(
            functools.partial(kernel, sizes),
            out_shape=shapes,
            in_specs=[pl.BlockSpec(memory_space=pltpu.SMEM)] * len(scalars)
            + [pl.BlockSpec(memory_space=space)] * len(arrays),
            out_specs=[pl.BlockSpec(memory_space=to)] * len(shapes),
            scratch_shapes=scratch,
            compiler_params=pltpu.CompilerParams(vmem_limit_bytes=limit),
            cost_estimate=pl.CostEstimate(flops=flops, bytes_accessed=nbytes, transcendentals=0),
            name=name,
        )(*scalars, *arrays)

    dims = (source, left_dims, right_dims)
    share, near_out, env_out = call(
        first_kernel,
        "first",
        [((secs, quarter, blk), BF16), ((2, half_rows, blk), BF16), ((3, half_rows, blk), BF16)],
        (),
        (source, wavefunction, left_env, right_env),
        [
            pltpu.SMEM(source.shape, source.dtype),
            pltpu.VMEM((secs, half_rows, blk), BF16),
            pltpu.VMEM((2, half_rows, blk), BF16),
            pltpu.SemaphoreType.DMA((6,)),
        ],
        space=pltpu.HBM,
        limit=VMEM_MOST,
    )
    mid = exchange(share, 2)
    near = exchange(near_out, 1)
    env_x = swap(env_out, "op")
    own_far = swap(wavefunction, "half")
    right_far = swap(right_env, "half")
    loaded = (after(wavefunction, env_out), left_env, right_env)
    own, left, right = call(
        load_kernel,
        "load",
        [(x.shape, x.dtype) for x in loaded],
        (),
        loaded,
        [pltpu.SemaphoreType.DMA((3,))],
        flops=FILL,
        space=pltpu.HBM,
        limit=VMEM_MUCH,
    )
    mid, near, env_x, own_far, right_far = (after(x, own) for x in (mid, near, env_x, own_far, right_far))
    envs = (left, right, right_far)

    far = exchange(mid, 1)
    (picked,) = call(pick_kernel, "pick", [((2, quarter, blk), BF16)], (source,), (mid,))
    mid_x = swap(picked, "op")
    (early,) = call(
        own_kernel,
        "own_slots",
        [((secs, half_rows, blk), F32)],
        dims,
        (own, after(own_far, picked), *envs),
        [pltpu.VMEM((blk, blk), BF16)],
        flops=FILL,
    )
    mid_far = swap(mid, "half")
    mid_x, env_x = after(mid_x, early), after(env_x, early)
    mid_x_far = swap(mid_x, "half")
    env_x_far = swap(after(env_x[:2], early), "half")
    far = after(far, early, mid_x_far, mid_far)
    near = after(near, mid_x)
    arrays = (
        near, swap(near, "half"), mid, mid_x, mid_far, mid_x_far, far, swap(far, "half"),
        *envs, env_x, env_x_far, early,
    )
    buffers = [pltpu.VMEM((secs, half_rows, half_rows), F32)]
    flops = 2 * 3 * half_rows * blk * blk * 2
    columns = (secs, half_rows, half_rows)
    (send,) = call(
        functools.partial(late_kernel, False), "late_sent", [(columns, BF16)], dims, arrays, buffers, flops
    )
    received = swap(send, "op")
    (keep,) = call(
        functools.partial(late_kernel, True), "late_kept", [(columns, F32)], dims, arrays, buffers, flops
    )
    (out,) = call(
        join_kernel,
        "join",
        [(columns, BF16)],
        (left_dims, right_dims),
        (keep, received),
        [pltpu.VMEM(columns, BF16), pltpu.SemaphoreType.DMA((secs,))],
        to=pltpu.HBM,
    )
    return out


def solution(mesh):
    shape = mesh.shape
    fits = (shape["sector"], shape["op"], shape["half"]) == (4, 2, 2)
    return jax.shard_map(
        four_by_two if fits else general,
        mesh=mesh,
        in_specs=(
            P(("group", "sector"), "half", None),
            P("op", ("group", "sector"), "half", None),
            P("op", ("group", "sector"), "half", None),
            P(None, "group"),
            P("group"),
            P("group"),
        ),
        out_specs=P(("group", "sector"), "half", "op"),
        check_vma=False,
    )
```

```python
import functools

import jax
import jax.numpy as jnp
from jax import lax
from jax.experimental import pallas as pl
from jax.experimental.pallas import tpu as pltpu
from jax.sharding import PartitionSpec as P

BF16 = jnp.bfloat16
F32 = jnp.float32
FILL = 30 * 10**9
VMEM_MOST = 61 * 1024 * 1024
VMEM_MUCH = 48 * 1024 * 1024
VMEM_LIMIT = 16 * 1024 * 1024


def general(wavefunction, left_env, right_env, source, left_dims, right_dims):
    sec_local, half_rows, blk_cols = wavefunction.shape
    pair_local = left_env.shape[0]
    needed = pair_local * sec_local
    sector_count = lax.axis_size("sector")
    sector_me = lax.axis_index("sector")
    op_me = lax.axis_index("op")
    half_me = lax.axis_index("half")
    places = sector_me * sec_local + jnp.arange(sec_local, dtype=jnp.int32)
    row_ids = half_me * half_rows + jnp.arange(half_rows, dtype=jnp.int32)
    col_ids = jnp.arange(blk_cols, dtype=jnp.int32)
    left_live = jnp.take(left_dims, places)
    right_live = jnp.take(right_dims, places)
    live_mask = (row_ids[None, :, None] < left_live[:, None, None]) & (
        col_ids[None, None, :] < right_live[:, None, None]
    )
    masked = jnp.where(live_mask, wavefunction, jnp.zeros((), wavefunction.dtype))
    wanted = lax.dynamic_slice(source, (op_me * pair_local, 0), (pair_local, source.shape[1]))
    wanted = (
        wanted.reshape(pair_local, sector_count, sec_local)
        .transpose(1, 0, 2)
        .reshape(sector_count, needed)
    )
    own_needs = lax.dynamic_index_in_dim(wanted, sector_me, 0, keepdims=False)
    capacity = -(-needed // sector_count)
    holders = wanted // sec_local
    is_mine = (holders == sector_me).astype(jnp.int32)
    earlier_hits = jnp.cumsum(is_mine, axis=1) - is_mine
    slot_ids = jnp.arange(capacity, dtype=jnp.int32)
    pick_mask = (is_mine[:, :, None] == 1) & (earlier_hits[:, :, None] == slot_ids[None, None, :])
    local_slot = jnp.sum(jnp.where(pick_mask, (wanted % sec_local)[:, :, None], 0), axis=1)
    outgoing = jnp.take(masked, local_slot.reshape(-1), axis=0).reshape(
        sector_count, capacity, half_rows, blk_cols
    )
    incoming = lax.all_to_all(outgoing, "sector", split_axis=0, concat_axis=0, tiled=True)
    owners = own_needs // sec_local
    same_owner = owners[:, None] == owners[None, :]
    order_ids = jnp.arange(needed, dtype=jnp.int32)
    earlier = order_ids[None, :] < order_ids[:, None]
    rank_of = jnp.sum((same_owner & earlier).astype(jnp.int32), axis=1)
    fetched = jnp.take(
        incoming.reshape(sector_count * capacity, half_rows, blk_cols),
        owners * capacity + rank_of,
        axis=0,
    )
    right_rows = right_env.reshape(needed, right_env.shape[2], blk_cols)
    right_part = jnp.einsum(
        "nab,ncb->nac",
        lax.all_gather(fetched, "half", axis=1, tiled=True),
        right_rows,
        preferred_element_type=F32,
    ).astype(BF16)
    right_part = right_part.reshape(pair_local, sec_local, right_part.shape[1], right_part.shape[2])
    partial_sum = jnp.einsum(
        "ksrc,kscj->srj",
        left_env,
        lax.all_gather(right_part, "half", axis=3, tiled=True),
        preferred_element_type=F32,
    )
    summed = lax.psum_scatter(partial_sum, "op", scatter_dimension=2, tiled=True)
    col_width = summed.shape[2]
    out_cols = op_me * col_width + jnp.arange(col_width, dtype=jnp.int32)
    out_mask = (row_ids[None, :, None] < left_live[:, None, None]) & (
        out_cols[None, None, :] < right_live[:, None, None]
    )
    return jnp.where(out_mask, summed, jnp.zeros((), F32)).astype(BF16)


def place():
    return lax.axis_index("sector"), lax.axis_index("op"), lax.axis_index("half")


def slots_of(sizes, source, z, op):
    pairs, secs = sizes[:2]
    found = []
    for n in range(pairs * secs):
        src = source[op * pairs + n // secs, z * secs + n % secs]
        holder = src // secs
        found.append((holder ^ z, src - holder * secs, src))
    return found


def ranked(slots, kind, rank):
    slot, local, source = jnp.int32(-1), jnp.int32(0), jnp.int32(0)
    seen = jnp.int32(0)
    for n, (k, b, s) in enumerate(slots):
        hit = (k == kind) & (seen == rank)
        slot = jnp.where(hit, n, slot)
        local = jnp.where(hit, b, local)
        source = jnp.where(hit, s, source)
        seen = seen + (k == kind).astype(jnp.int32)
    return slot, local, source


def first_kernel(sizes, source_hbm, own, left, right, share, near_out, env_out, source, own_buf, left_buf, sem):
    pairs, secs, half_rows, blk = sizes
    quarter = half_rows // 2
    z, o, _ = place()
    copies = [pltpu.make_async_copy(source_hbm, source, sem.at[0]), pltpu.make_async_copy(own, own_buf, sem.at[1])]
    for copy in copies:
        copy.start()
    copies[0].wait()
    mine = slots_of(sizes, source, z, o)
    for j in range(2):
        n = jnp.maximum(ranked(mine, 3, j)[0], 0)
        for src, dst in ((right, env_out.at[j]), (left, left_buf.at[j])):
            copy = pltpu.make_async_copy(src.at[n // secs, n % secs], dst, sem.at[len(copies)])
            copy.start()
            copies.append(copy)
    theirs = slots_of(sizes, source, z ^ 1, o)
    copies[1].wait()
    share[...] = own_buf[:, pl.ds(pl.multiple_of(o * quarter, quarter), quarter)]
    for j in range(2):
        near_out[j] = own_buf[ranked(theirs, 1, j)[1]]
    for copy in copies[2:]:
        copy.wait()
    for j in range(2):
        for part in range(2):
            first = pl.multiple_of(part * half_rows + (1 - o) * quarter, quarter)
            to = j * half_rows + part * quarter
            env_out[2, :, to : to + quarter] = left_buf[j, :, pl.ds(first, quarter)]


def load_kernel(sizes, *refs):
    count = len(refs) // 2
    copies = [pltpu.make_async_copy(refs[i], refs[count + i], refs[-1].at[i]) for i in range(count)]
    for copy in copies:
        copy.start()
    for copy in copies:
        copy.wait()


def pick_kernel(sizes, source, mid, picked):
    z, o, _ = place()
    theirs = slots_of(sizes, source, z, 1 - o)
    for j in range(2):
        picked[j] = mid[ranked(theirs, 2, j)[1]]


def live_columns(sizes, right_dims, src):
    col = lax.broadcasted_iota(jnp.int32, (1, sizes[3]), 1)
    return (col < right_dims[src]).astype(F32).astype(BF16)


def times_right(m, r, row, left_live):
    part = lax.dot_general(m, r, (((1,), (1,)), ((), ())), preferred_element_type=F32)
    return jnp.where(row < left_live, part, 0.0).astype(BF16)


def own_kernel(sizes, source, left_dims, right_dims, own, own_far, left, right, right_far, acc, m_buf):
    pairs, secs, half_rows, blk = sizes
    z, o, h = place()
    slots = slots_of(sizes, source, z, o)
    acc[...] = jnp.zeros_like(acc)
    row = lax.broadcasted_iota(jnp.int32, (blk, 1), 0)
    for j in range(2):
        n, local, src = ranked(slots, 0, j)

        @pl.when(n >= 0)
        def _():
            k, t = n // secs, n % secs
            live = live_columns(sizes, right_dims, src)
            for half, ref in ((h, own), (1 - h, own_far)):
                m_buf[pl.ds(pl.multiple_of(half * half_rows, half_rows), half_rows)] = ref[local] * live
            r = jnp.concatenate(
                [jnp.where(h == 0, right[k, t], right_far[k, t]), jnp.where(h == 0, right_far[k, t], right[k, t])],
                axis=0,
            )
            part = times_right(m_buf[...], r, row, left_dims[src])
            acc[t] += jnp.dot(left[k, t], part, preferred_element_type=F32)


def late_kernel(
    kept, sizes, source, left_dims, right_dims, near, near_far, mid, mid_x, mid_far, mid_x_far, far, far_far,
    left, right, right_far, env_x, env_x_far, early, out, total,
):
    pairs, secs, half_rows, blk = sizes
    quarter = half_rows // 2
    z, o, h = place()
    mine = slots_of(sizes, source, z, o)
    theirs = slots_of(sizes, source, z, 1 - o)
    side = o if kept else 1 - o
    total[...] = early[:, :, pl.ds(pl.multiple_of(side * half_rows, half_rows), half_rows)]
    parts = []

    def add(slot, pieces, firsts, env=None):
        n, _, src = slot
        k, t = jnp.maximum(n, 0) // secs, jnp.maximum(n, 0) % secs
        size = pieces[0].shape[0]
        if env is None:
            r = jnp.where(side == h, right[k, t], right_far[k, t])
            lefts = [left[k, t, :, pl.ds(pl.multiple_of(first, size), size)] for first in firsts]
        else:
            r = jnp.where(side == h, env_x[env], env_x_far[env])
            lefts = [
                env_x[2, :, pl.ds(pl.multiple_of(env * half_rows + half * quarter, quarter), quarter)]
                for half in (h, 1 - h)
            ]
        at = lax.broadcasted_iota(jnp.int32, (size, 1), 0)
        row = jnp.concatenate([at + first for first in firsts], axis=0)
        live = live_columns(sizes, right_dims, src)
        left_live = jnp.where(n >= 0, left_dims[src], 0)
        part = times_right(jnp.concatenate(pieces, axis=0), r * live, row, left_live)
        parts.append((t, jnp.concatenate(lefts, axis=1), part))

    halves = [h * half_rows, (1 - h) * half_rows]
    ops = [o * quarter, (1 - o) * quarter]
    for j in range(2):
        add(ranked(mine, 1, j), [near[j], near_far[j]], halves)
        slot = ranked(mine, 2, j)
        pieces = [mid[slot[1]], mid_x[j], mid_far[slot[1]], mid_x_far[j]]
        add(slot, pieces, [half + op for half in halves for op in ops])
        for slot, env in ((ranked(mine, 3, j), None), (ranked(theirs, 3, j), j)):
            add(slot, [far[slot[1]], far_far[slot[1]]], [half + ops[0] for half in halves], env)
    for t, l, part in parts:
        total[t] += jnp.dot(l, part, preferred_element_type=F32)
    out[...] = total[...].astype(out.dtype)


def join_kernel(sizes, left_dims, right_dims, keep, received, out, held, sem):
    secs, half_rows, blk = sizes[1:]
    z, o, h = place()
    row = h * half_rows + lax.broadcasted_iota(jnp.int32, (half_rows, 1), 0)
    col = o * half_rows + lax.broadcasted_iota(jnp.int32, (1, half_rows), 1)
    copies = [pltpu.make_async_copy(held.at[t], out.at[t], sem.at[t]) for t in range(secs)]
    for t in range(secs):
        live = (row < left_dims[z * secs + t]) & (col < right_dims[z * secs + t])
        held[t] = jnp.where(live, keep[t] + received[t].astype(F32), 0.0).astype(BF16)
        copies[t].start()
    for copy in copies:
        copy.wait()


def swap(x, axis):
    return lax.ppermute(x, axis, [(0, 1), (1, 0)])


def after(x, *earlier):
    return lax.optimization_barrier((x, *earlier))[0]


def exchange(x, kind):
    return lax.ppermute(x, "sector", [(i, i ^ kind) for i in range(4)])


def four_by_two(wavefunction, left_env, right_env, source, left_dims, right_dims):
    secs, half_rows, blk = wavefunction.shape
    pairs = left_env.shape[0]
    quarter = half_rows // 2
    sizes = (pairs, secs, half_rows, blk)

    def call(
        kernel, name, outs, scalars, arrays, scratch=(), flops=0, space=pltpu.VMEM, limit=VMEM_LIMIT, to=pltpu.VMEM
    ):
        shapes = [jax.ShapeDtypeStruct(shape, dtype) for shape, dtype in outs]
        nbytes = sum(s.size * s.dtype.itemsize for s in [*shapes, *arrays])
        return pl.pallas_call(
            functools.partial(kernel, sizes),
            out_shape=shapes,
            in_specs=[pl.BlockSpec(memory_space=pltpu.SMEM)] * len(scalars)
            + [pl.BlockSpec(memory_space=space)] * len(arrays),
            out_specs=[pl.BlockSpec(memory_space=to)] * len(shapes),
            scratch_shapes=scratch,
            compiler_params=pltpu.CompilerParams(vmem_limit_bytes=limit),
            cost_estimate=pl.CostEstimate(flops=flops, bytes_accessed=nbytes, transcendentals=0),
            name=name,
        )(*scalars, *arrays)

    dims = (source, left_dims, right_dims)
    share, near_out, env_out = call(
        first_kernel,
        "first",
        [((secs, quarter, blk), BF16), ((2, half_rows, blk), BF16), ((3, half_rows, blk), BF16)],
        (),
        (source, wavefunction, left_env, right_env),
        [
            pltpu.SMEM(source.shape, source.dtype),
            pltpu.VMEM((secs, half_rows, blk), BF16),
            pltpu.VMEM((2, half_rows, blk), BF16),
            pltpu.SemaphoreType.DMA((6,)),
        ],
        space=pltpu.HBM,
        limit=VMEM_MOST,
    )
    mid = exchange(share, 2)
    near = exchange(near_out, 1)
    env_x = swap(env_out, "op")
    own_far = swap(after(wavefunction, share), "half")
    right_far = swap(after(right_env, share), "half")
    loaded = (after(wavefunction, env_out), left_env, right_env)
    own, left, right = call(
        load_kernel,
        "load",
        [(x.shape, x.dtype) for x in loaded],
        (),
        loaded,
        [pltpu.SemaphoreType.DMA((3,))],
        flops=FILL,
        space=pltpu.HBM,
        limit=VMEM_MUCH,
    )
    mid, near, env_x, own_far, right_far = (after(x, own) for x in (mid, near, env_x, own_far, right_far))
    envs = (left, right, right_far)

    far = exchange(mid, 1)
    (picked,) = call(pick_kernel, "pick", [((2, quarter, blk), BF16)], (source,), (mid,))
    mid_x = swap(picked, "op")
    (early,) = call(
        own_kernel,
        "own_slots",
        [((secs, half_rows, blk), F32)],
        dims,
        (own, after(own_far, picked), *envs),
        [pltpu.VMEM((blk, blk), BF16)],
        flops=FILL,
    )
    mid_far = swap(mid, "half")
    mid_x, env_x = after(mid_x, early), after(env_x, early)
    mid_x_far = swap(mid_x, "half")
    env_x_far = swap(after(env_x[:2], early), "half")
    far = after(far, early, mid_x_far, mid_far)
    near = after(near, mid_x)
    arrays = (
        near, swap(near, "half"), mid, mid_x, mid_far, mid_x_far, far, swap(far, "half"),
        *envs, env_x, env_x_far, early,
    )
    buffers = [pltpu.VMEM((secs, half_rows, half_rows), F32)]
    flops = 2 * 3 * half_rows * blk * blk * 2
    columns = (secs, half_rows, half_rows)
    (send,) = call(
        functools.partial(late_kernel, False), "late_sent", [(columns, BF16)], dims, arrays, buffers, flops
    )
    received = swap(send, "op")
    (keep,) = call(
        functools.partial(late_kernel, True), "late_kept", [(columns, F32)], dims, arrays, buffers, flops
    )
    (out,) = call(
        join_kernel,
        "join",
        [(columns, BF16)],
        (left_dims, right_dims),
        (keep, received),
        [pltpu.VMEM(columns, BF16), pltpu.SemaphoreType.DMA((secs,))],
        to=pltpu.HBM,
    )
    return out


def solution(mesh):
    shape = mesh.shape
    fits = (shape["sector"], shape["op"], shape["half"]) == (4, 2, 2)
    return jax.shard_map(
        four_by_two if fits else general,
        mesh=mesh,
        in_specs=(
            P(("group", "sector"), "half", None),
            P("op", ("group", "sector"), "half", None),
            P("op", ("group", "sector"), "half", None),
            P(None, "group"),
            P("group"),
            P("group"),
        ),
        out_specs=P(("group", "sector"), "half", "op"),
        check_vma=False,
    )
```

```python
import functools

import jax
import jax.numpy as jnp
from jax import lax
from jax.experimental import pallas as pl
from jax.experimental.pallas import tpu as pltpu
from jax.sharding import PartitionSpec as P

BF16 = jnp.bfloat16
F32 = jnp.float32
FILL = 30 * 10**9
VMEM_MOST = 61 * 1024 * 1024
VMEM_MUCH = 48 * 1024 * 1024
VMEM_LIMIT = 16 * 1024 * 1024


def general(wavefunction, left_env, right_env, source, left_dims, right_dims):
    sec_local, half_rows, blk_cols = wavefunction.shape
    pair_local = left_env.shape[0]
    needed = pair_local * sec_local
    sector_count = lax.axis_size("sector")
    sector_me = lax.axis_index("sector")
    op_me = lax.axis_index("op")
    half_me = lax.axis_index("half")
    places = sector_me * sec_local + jnp.arange(sec_local, dtype=jnp.int32)
    row_ids = half_me * half_rows + jnp.arange(half_rows, dtype=jnp.int32)
    col_ids = jnp.arange(blk_cols, dtype=jnp.int32)
    left_live = jnp.take(left_dims, places)
    right_live = jnp.take(right_dims, places)
    live_mask = (row_ids[None, :, None] < left_live[:, None, None]) & (
        col_ids[None, None, :] < right_live[:, None, None]
    )
    masked = jnp.where(live_mask, wavefunction, jnp.zeros((), wavefunction.dtype))
    wanted = lax.dynamic_slice(source, (op_me * pair_local, 0), (pair_local, source.shape[1]))
    wanted = (
        wanted.reshape(pair_local, sector_count, sec_local)
        .transpose(1, 0, 2)
        .reshape(sector_count, needed)
    )
    own_needs = lax.dynamic_index_in_dim(wanted, sector_me, 0, keepdims=False)
    capacity = -(-needed // sector_count)
    holders = wanted // sec_local
    is_mine = (holders == sector_me).astype(jnp.int32)
    earlier_hits = jnp.cumsum(is_mine, axis=1) - is_mine
    slot_ids = jnp.arange(capacity, dtype=jnp.int32)
    pick_mask = (is_mine[:, :, None] == 1) & (earlier_hits[:, :, None] == slot_ids[None, None, :])
    local_slot = jnp.sum(jnp.where(pick_mask, (wanted % sec_local)[:, :, None], 0), axis=1)
    outgoing = jnp.take(masked, local_slot.reshape(-1), axis=0).reshape(
        sector_count, capacity, half_rows, blk_cols
    )
    incoming = lax.all_to_all(outgoing, "sector", split_axis=0, concat_axis=0, tiled=True)
    owners = own_needs // sec_local
    same_owner = owners[:, None] == owners[None, :]
    order_ids = jnp.arange(needed, dtype=jnp.int32)
    earlier = order_ids[None, :] < order_ids[:, None]
    rank_of = jnp.sum((same_owner & earlier).astype(jnp.int32), axis=1)
    fetched = jnp.take(
        incoming.reshape(sector_count * capacity, half_rows, blk_cols),
        owners * capacity + rank_of,
        axis=0,
    )
    right_rows = right_env.reshape(needed, right_env.shape[2], blk_cols)
    right_part = jnp.einsum(
        "nab,ncb->nac",
        lax.all_gather(fetched, "half", axis=1, tiled=True),
        right_rows,
        preferred_element_type=F32,
    ).astype(BF16)
    right_part = right_part.reshape(pair_local, sec_local, right_part.shape[1], right_part.shape[2])
    partial_sum = jnp.einsum(
        "ksrc,kscj->srj",
        left_env,
        lax.all_gather(right_part, "half", axis=3, tiled=True),
        preferred_element_type=F32,
    )
    summed = lax.psum_scatter(partial_sum, "op", scatter_dimension=2, tiled=True)
    col_width = summed.shape[2]
    out_cols = op_me * col_width + jnp.arange(col_width, dtype=jnp.int32)
    out_mask = (row_ids[None, :, None] < left_live[:, None, None]) & (
        out_cols[None, None, :] < right_live[:, None, None]
    )
    return jnp.where(out_mask, summed, jnp.zeros((), F32)).astype(BF16)


def place():
    return lax.axis_index("sector"), lax.axis_index("op"), lax.axis_index("half")


def slots_of(sizes, source, z, op):
    pairs, secs = sizes[:2]
    found = []
    for n in range(pairs * secs):
        src = source[op * pairs + n // secs, z * secs + n % secs]
        holder = src // secs
        found.append((holder ^ z, src - holder * secs, src))
    return found


def ranked(slots, kind, rank):
    slot, local, source = jnp.int32(-1), jnp.int32(0), jnp.int32(0)
    seen = jnp.int32(0)
    for n, (k, b, s) in enumerate(slots):
        hit = (k == kind) & (seen == rank)
        slot = jnp.where(hit, n, slot)
        local = jnp.where(hit, b, local)
        source = jnp.where(hit, s, source)
        seen = seen + (k == kind).astype(jnp.int32)
    return slot, local, source


def first_kernel(sizes, source_hbm, own, left, right, share, near_out, env_out, source, own_buf, left_buf, sem):
    pairs, secs, half_rows, blk = sizes
    quarter = half_rows // 2
    z, o, _ = place()
    copies = [pltpu.make_async_copy(source_hbm, source, sem.at[0]), pltpu.make_async_copy(own, own_buf, sem.at[1])]
    for copy in copies:
        copy.start()
    copies[0].wait()
    mine = slots_of(sizes, source, z, o)
    for j in range(2):
        n = jnp.maximum(ranked(mine, 3, j)[0], 0)
        for src, dst in ((right, env_out.at[j]), (left, left_buf.at[j])):
            copy = pltpu.make_async_copy(src.at[n // secs, n % secs], dst, sem.at[len(copies)])
            copy.start()
            copies.append(copy)
    theirs = slots_of(sizes, source, z ^ 1, o)
    copies[1].wait()
    share[...] = own_buf[:, pl.ds(pl.multiple_of(o * quarter, quarter), quarter)]
    for j in range(2):
        near_out[j] = own_buf[ranked(theirs, 1, j)[1]]
    for copy in copies[2:]:
        copy.wait()
    for j in range(2):
        for part in range(2):
            first = pl.multiple_of(part * half_rows + (1 - o) * quarter, quarter)
            to = j * half_rows + part * quarter
            env_out[2, :, to : to + quarter] = left_buf[j, :, pl.ds(first, quarter)]


def load_kernel(sizes, *refs):
    count = len(refs) // 2
    copies = [pltpu.make_async_copy(refs[i], refs[count + i], refs[-1].at[i]) for i in range(count)]
    for copy in copies:
        copy.start()
    for copy in copies:
        copy.wait()


def pick_kernel(sizes, source, mid, picked):
    z, o, _ = place()
    theirs = slots_of(sizes, source, z, 1 - o)
    for j in range(2):
        picked[j] = mid[ranked(theirs, 2, j)[1]]


def live_columns(sizes, right_dims, src):
    col = lax.broadcasted_iota(jnp.int32, (1, sizes[3]), 1)
    return (col < right_dims[src]).astype(F32).astype(BF16)


def times_right(m, r, row, left_live):
    part = lax.dot_general(m, r, (((1,), (1,)), ((), ())), preferred_element_type=F32)
    return jnp.where(row < left_live, part, 0.0).astype(BF16)


def own_kernel(sizes, source, left_dims, right_dims, own, own_far, left, right, right_far, acc, m_buf):
    pairs, secs, half_rows, blk = sizes
    z, o, h = place()
    slots = slots_of(sizes, source, z, o)
    acc[...] = jnp.zeros_like(acc)
    row = lax.broadcasted_iota(jnp.int32, (blk, 1), 0)
    for j in range(2):
        n, local, src = ranked(slots, 0, j)

        @pl.when(n >= 0)
        def _():
            k, t = n // secs, n % secs
            live = live_columns(sizes, right_dims, src)
            for half, ref in ((h, own), (1 - h, own_far)):
                m_buf[pl.ds(pl.multiple_of(half * half_rows, half_rows), half_rows)] = ref[local] * live
            r = jnp.concatenate(
                [jnp.where(h == 0, right[k, t], right_far[k, t]), jnp.where(h == 0, right_far[k, t], right[k, t])],
                axis=0,
            )
            part = times_right(m_buf[...], r, row, left_dims[src])
            acc[t] += jnp.dot(left[k, t], part, preferred_element_type=F32)


class Late:
    def __init__(self, sizes, dims, side, left, right, right_far):
        self.sizes, self.dims, self.side = sizes, dims, side
        self.left, self.right, self.right_far = left, right, right_far
        z, self.o, self.h = place()
        self.mine = slots_of(sizes, dims[0], z, self.o)
        self.theirs = slots_of(sizes, dims[0], z, 1 - self.o)
        quarter = sizes[2] // 2
        self.halves = [self.h * sizes[2], (1 - self.h) * sizes[2]]
        self.ops = [self.o * quarter, (1 - self.o) * quarter]
        self.parts = []

    def target(self, n):
        n = jnp.maximum(n, 0)
        return n // self.sizes[1], n % self.sizes[1]

    def sided(self, mine, far):
        return jnp.where(self.side == self.h, mine, far)

    def add(self, slot, pieces, firsts, r, lefts):
        n, _, src = slot
        at = lax.broadcasted_iota(jnp.int32, (pieces[0].shape[0], 1), 0)
        row = jnp.concatenate([at + first for first in firsts], axis=0)
        left_live = jnp.where(n >= 0, self.dims[1][src], 0)
        live = live_columns(self.sizes, self.dims[2], src)
        part = times_right(jnp.concatenate(pieces, axis=0), r * live, row, left_live)
        self.parts.append((self.target(n)[1], jnp.concatenate(lefts, axis=1), part))

    def add_own(self, slot, pieces, firsts):
        k, t = self.target(slot[0])
        size = pieces[0].shape[0]
        lefts = [self.left[k, t, :, pl.ds(pl.multiple_of(first, size), size)] for first in firsts]
        self.add(slot, pieces, firsts, self.sided(self.right[k, t], self.right_far[k, t]), lefts)

    def add_near(self, near, near_far):
        for j in range(2):
            self.add_own(ranked(self.mine, 1, j), [near[j], near_far[j]], self.halves)

    def add_mid(self, mid, mid_x, mid_far, mid_x_far):
        for j in range(2):
            slot = ranked(self.mine, 2, j)
            pieces = [mid[slot[1]], mid_x[j], mid_far[slot[1]], mid_x_far[j]]
            self.add_own(slot, pieces, [half + op for half in self.halves for op in self.ops])

    def add_far(self, far, far_far, env_x, env_x_far):
        half_rows = self.sizes[2]
        quarter = half_rows // 2
        firsts = [half + self.ops[0] for half in self.halves]
        for j in range(2):
            slot = ranked(self.mine, 3, j)
            self.add_own(slot, [far[slot[1]], far_far[slot[1]]], firsts)
            slot = ranked(self.theirs, 3, j)
            lefts = [
                env_x[2, :, pl.ds(pl.multiple_of(j * half_rows + half * quarter, quarter), quarter)]
                for half in (self.h, 1 - self.h)
            ]
            r = self.sided(env_x[j], env_x_far[j])
            self.add(slot, [far[slot[1]], far_far[slot[1]]], firsts, r, lefts)

    def sum_into(self, total):
        for t, left, part in self.parts:
            total[t] += jnp.dot(left, part, preferred_element_type=F32)


def begin_kernel(kept, sizes, source, left_dims, right_dims, *refs):
    near, mid, envs, early, total = refs[:2], refs[2:6], refs[6:9], refs[9], refs[10]
    o = place()[1]
    side, half_rows = (o if kept else 1 - o), sizes[2]
    total[...] = early[:, :, pl.ds(pl.multiple_of(side * half_rows, half_rows), half_rows)]
    late = Late(sizes, (source, left_dims, right_dims), side, *envs)
    late.add_near(*near)
    late.add_mid(*mid)
    late.sum_into(total)


def finish_kernel(kept, sizes, source, left_dims, right_dims, *refs):
    fars, envs, begun, out, total = refs[:4], refs[4:7], refs[7], refs[8], refs[9]
    o = place()[1]
    total[...] = begun[...]
    late = Late(sizes, (source, left_dims, right_dims), o if kept else 1 - o, *envs)
    late.add_far(*fars)
    late.sum_into(total)
    out[...] = total[...].astype(out.dtype)


def join_kernel(sizes, left_dims, right_dims, keep, received, out, held, sem):
    secs, half_rows, blk = sizes[1:]
    z, o, h = place()
    row = h * half_rows + lax.broadcasted_iota(jnp.int32, (half_rows, 1), 0)
    col = o * half_rows + lax.broadcasted_iota(jnp.int32, (1, half_rows), 1)
    copies = [pltpu.make_async_copy(held.at[t], out.at[t], sem.at[t]) for t in range(secs)]
    for t in range(secs):
        live = (row < left_dims[z * secs + t]) & (col < right_dims[z * secs + t])
        held[t] = jnp.where(live, keep[t] + received[t].astype(F32), 0.0).astype(BF16)
        copies[t].start()
    for copy in copies:
        copy.wait()


def swap(x, axis):
    return lax.ppermute(x, axis, [(0, 1), (1, 0)])


def after(x, *earlier):
    return lax.optimization_barrier((x, *earlier))[0]


def exchange(x, kind):
    return lax.ppermute(x, "sector", [(i, i ^ kind) for i in range(4)])


def four_by_two(wavefunction, left_env, right_env, source, left_dims, right_dims):
    secs, half_rows, blk = wavefunction.shape
    pairs = left_env.shape[0]
    quarter = half_rows // 2
    sizes = (pairs, secs, half_rows, blk)

    def call(
        kernel, name, outs, scalars, arrays, scratch=(), flops=0, space=pltpu.VMEM, limit=VMEM_LIMIT, to=pltpu.VMEM
    ):
        shapes = [jax.ShapeDtypeStruct(shape, dtype) for shape, dtype in outs]
        nbytes = sum(s.size * s.dtype.itemsize for s in [*shapes, *arrays])
        return pl.pallas_call(
            functools.partial(kernel, sizes),
            out_shape=shapes,
            in_specs=[pl.BlockSpec(memory_space=pltpu.SMEM)] * len(scalars)
            + [pl.BlockSpec(memory_space=space)] * len(arrays),
            out_specs=[pl.BlockSpec(memory_space=to)] * len(shapes),
            scratch_shapes=scratch,
            compiler_params=pltpu.CompilerParams(vmem_limit_bytes=limit),
            cost_estimate=pl.CostEstimate(flops=flops, bytes_accessed=nbytes, transcendentals=0),
            name=name,
        )(*scalars, *arrays)

    dims = (source, left_dims, right_dims)
    share, near_out, env_out = call(
        first_kernel,
        "first",
        [((secs, quarter, blk), BF16), ((2, half_rows, blk), BF16), ((3, half_rows, blk), BF16)],
        (),
        (source, wavefunction, left_env, right_env),
        [
            pltpu.SMEM(source.shape, source.dtype),
            pltpu.VMEM((secs, half_rows, blk), BF16),
            pltpu.VMEM((2, half_rows, blk), BF16),
            pltpu.SemaphoreType.DMA((6,)),
        ],
        space=pltpu.HBM,
        limit=VMEM_MOST,
    )
    mid = exchange(share, 2)
    near = exchange(near_out, 1)
    env_x = swap(env_out, "op")
    own_far = swap(after(wavefunction, near_out), "half")
    right_far = swap(after(right_env, env_out), "half")
    loaded = (after(wavefunction, env_out), left_env, right_env)
    own, left, right = call(
        load_kernel,
        "load",
        [(x.shape, x.dtype) for x in loaded],
        (),
        loaded,
        [pltpu.SemaphoreType.DMA((3,))],
        flops=FILL,
        space=pltpu.HBM,
        limit=VMEM_MUCH,
    )
    mid, near, env_x, own_far, right_far = (after(x, own) for x in (mid, near, env_x, own_far, right_far))
    envs = (left, right, right_far)

    far = exchange(mid, 1)
    (picked,) = call(pick_kernel, "pick", [((2, quarter, blk), BF16)], (source,), (mid,))
    mid_x = swap(picked, "op")
    (early,) = call(
        own_kernel,
        "own_slots",
        [((secs, half_rows, blk), F32)],
        dims,
        (own, after(own_far, picked), *envs),
        [pltpu.VMEM((blk, blk), BF16)],
        flops=FILL,
    )
    mid_far = swap(after(mid, early), "half")
    mid_x, env_x = after(mid_x, early), after(env_x, early)
    mid_x_far = swap(mid_x, "half")
    env_x_far = swap(after(env_x[:2], early), "half")
    far = after(far, early, mid_x_far, mid_far)
    near = after(near, mid_x)
    arrivals = (near, swap(near, "half"), mid, mid_x, mid_far, mid_x_far)
    fars = (far, swap(far, "half"), env_x, env_x_far)
    columns = (secs, half_rows, half_rows)

    def side(kept, dtype, fill):
        (begun,) = call(
            functools.partial(begin_kernel, kept), "begin", [(columns, F32)], dims, (*arrivals, *envs, early), flops=fill
        )
        return call(
            functools.partial(finish_kernel, kept),
            "finish",
            [(columns, dtype)],
            dims,
            (*fars, *envs, begun),
            [pltpu.VMEM(columns, F32)],
        )[0]

    received = swap(side(False, BF16, 0), "op")
    keep = side(True, F32, 0)
    (out,) = call(
        join_kernel,
        "join",
        [(columns, BF16)],
        (left_dims, right_dims),
        (keep, received),
        [pltpu.VMEM(columns, BF16), pltpu.SemaphoreType.DMA((secs,))],
        to=pltpu.HBM,
    )
    return out


def solution(mesh):
    shape = mesh.shape
    fits = (shape["sector"], shape["op"], shape["half"]) == (4, 2, 2)
    return jax.shard_map(
        four_by_two if fits else general,
        mesh=mesh,
        in_specs=(
            P(("group", "sector"), "half", None),
            P("op", ("group", "sector"), "half", None),
            P("op", ("group", "sector"), "half", None),
            P(None, "group"),
            P("group"),
            P("group"),
        ),
        out_specs=P(("group", "sector"), "half", "op"),
        check_vma=False,
    )
```

```python
import functools

import jax
import jax.numpy as jnp
from jax import lax
from jax.experimental import pallas as pl
from jax.experimental.pallas import tpu as pltpu
from jax.sharding import PartitionSpec as P

BF16 = jnp.bfloat16
F32 = jnp.float32
FILL = 30 * 10**9
VMEM_MOST = 61 * 1024 * 1024
VMEM_MUCH = 48 * 1024 * 1024
VMEM_LIMIT = 16 * 1024 * 1024


def general(wavefunction, left_env, right_env, source, left_dims, right_dims):
    sec_local, half_rows, blk_cols = wavefunction.shape
    pair_local = left_env.shape[0]
    needed = pair_local * sec_local
    sector_count = lax.axis_size("sector")
    sector_me = lax.axis_index("sector")
    op_me = lax.axis_index("op")
    half_me = lax.axis_index("half")
    places = sector_me * sec_local + jnp.arange(sec_local, dtype=jnp.int32)
    row_ids = half_me * half_rows + jnp.arange(half_rows, dtype=jnp.int32)
    col_ids = jnp.arange(blk_cols, dtype=jnp.int32)
    left_live = jnp.take(left_dims, places)
    right_live = jnp.take(right_dims, places)
    live_mask = (row_ids[None, :, None] < left_live[:, None, None]) & (
        col_ids[None, None, :] < right_live[:, None, None]
    )
    masked = jnp.where(live_mask, wavefunction, jnp.zeros((), wavefunction.dtype))
    wanted = lax.dynamic_slice(source, (op_me * pair_local, 0), (pair_local, source.shape[1]))
    wanted = (
        wanted.reshape(pair_local, sector_count, sec_local)
        .transpose(1, 0, 2)
        .reshape(sector_count, needed)
    )
    own_needs = lax.dynamic_index_in_dim(wanted, sector_me, 0, keepdims=False)
    capacity = -(-needed // sector_count)
    holders = wanted // sec_local
    is_mine = (holders == sector_me).astype(jnp.int32)
    earlier_hits = jnp.cumsum(is_mine, axis=1) - is_mine
    slot_ids = jnp.arange(capacity, dtype=jnp.int32)
    pick_mask = (is_mine[:, :, None] == 1) & (earlier_hits[:, :, None] == slot_ids[None, None, :])
    local_slot = jnp.sum(jnp.where(pick_mask, (wanted % sec_local)[:, :, None], 0), axis=1)
    outgoing = jnp.take(masked, local_slot.reshape(-1), axis=0).reshape(
        sector_count, capacity, half_rows, blk_cols
    )
    incoming = lax.all_to_all(outgoing, "sector", split_axis=0, concat_axis=0, tiled=True)
    owners = own_needs // sec_local
    same_owner = owners[:, None] == owners[None, :]
    order_ids = jnp.arange(needed, dtype=jnp.int32)
    earlier = order_ids[None, :] < order_ids[:, None]
    rank_of = jnp.sum((same_owner & earlier).astype(jnp.int32), axis=1)
    fetched = jnp.take(
        incoming.reshape(sector_count * capacity, half_rows, blk_cols),
        owners * capacity + rank_of,
        axis=0,
    )
    right_rows = right_env.reshape(needed, right_env.shape[2], blk_cols)
    right_part = jnp.einsum(
        "nab,ncb->nac",
        lax.all_gather(fetched, "half", axis=1, tiled=True),
        right_rows,
        preferred_element_type=F32,
    ).astype(BF16)
    right_part = right_part.reshape(pair_local, sec_local, right_part.shape[1], right_part.shape[2])
    partial_sum = jnp.einsum(
        "ksrc,kscj->srj",
        left_env,
        lax.all_gather(right_part, "half", axis=3, tiled=True),
        preferred_element_type=F32,
    )
    summed = lax.psum_scatter(partial_sum, "op", scatter_dimension=2, tiled=True)
    col_width = summed.shape[2]
    out_cols = op_me * col_width + jnp.arange(col_width, dtype=jnp.int32)
    out_mask = (row_ids[None, :, None] < left_live[:, None, None]) & (
        out_cols[None, None, :] < right_live[:, None, None]
    )
    return jnp.where(out_mask, summed, jnp.zeros((), F32)).astype(BF16)


def place():
    return lax.axis_index("sector"), lax.axis_index("op"), lax.axis_index("half")


def slots_of(sizes, source, z, op):
    pairs, secs = sizes[:2]
    found = []
    for n in range(pairs * secs):
        src = source[op * pairs + n // secs, z * secs + n % secs]
        holder = src // secs
        found.append((holder ^ z, src - holder * secs, src))
    return found


def ranked(slots, kind, rank):
    slot, local, source = jnp.int32(-1), jnp.int32(0), jnp.int32(0)
    seen = jnp.int32(0)
    for n, (k, b, s) in enumerate(slots):
        hit = (k == kind) & (seen == rank)
        slot = jnp.where(hit, n, slot)
        local = jnp.where(hit, b, local)
        source = jnp.where(hit, s, source)
        seen = seen + (k == kind).astype(jnp.int32)
    return slot, local, source


def first_kernel(sizes, source_hbm, own, left, right, share, near_out, env_out, source, own_buf, left_buf, sem):
    pairs, secs, half_rows, blk = sizes
    quarter = half_rows // 2
    z, o, _ = place()
    copies = [pltpu.make_async_copy(source_hbm, source, sem.at[0]), pltpu.make_async_copy(own, own_buf, sem.at[1])]
    for copy in copies:
        copy.start()
    copies[0].wait()
    mine = slots_of(sizes, source, z, o)
    for j in range(2):
        n = jnp.maximum(ranked(mine, 3, j)[0], 0)
        for src, dst in ((right, env_out.at[j]), (left, left_buf.at[j])):
            copy = pltpu.make_async_copy(src.at[n // secs, n % secs], dst, sem.at[len(copies)])
            copy.start()
            copies.append(copy)
    theirs = slots_of(sizes, source, z ^ 1, o)
    copies[1].wait()
    share[...] = own_buf[:, pl.ds(pl.multiple_of(o * quarter, quarter), quarter)]
    for j in range(2):
        near_out[j] = own_buf[ranked(theirs, 1, j)[1]]
    for copy in copies[2:]:
        copy.wait()
    for j in range(2):
        for part in range(2):
            first = pl.multiple_of(part * half_rows + (1 - o) * quarter, quarter)
            to = j * half_rows + part * quarter
            env_out[2, :, to : to + quarter] = left_buf[j, :, pl.ds(first, quarter)]


def load_kernel(sizes, *refs):
    count = len(refs) // 2
    copies = [pltpu.make_async_copy(refs[i], refs[count + i], refs[-1].at[i]) for i in range(count)]
    for copy in copies:
        copy.start()
    for copy in copies:
        copy.wait()


def pick_kernel(sizes, source, mid, picked):
    z, o, _ = place()
    theirs = slots_of(sizes, source, z, 1 - o)
    for j in range(2):
        picked[j] = mid[ranked(theirs, 2, j)[1]]


def live_columns(sizes, right_dims, src):
    col = lax.broadcasted_iota(jnp.int32, (1, sizes[3]), 1)
    return (col < right_dims[src]).astype(F32).astype(BF16)


def times_right(m, r, row, left_live):
    part = lax.dot_general(m, r, (((1,), (1,)), ((), ())), preferred_element_type=F32)
    return jnp.where(row < left_live, part, 0.0).astype(BF16)


def own_kernel(sizes, source, left_dims, right_dims, own, own_far, left, right, right_far, acc, m_buf):
    pairs, secs, half_rows, blk = sizes
    z, o, h = place()
    slots = slots_of(sizes, source, z, o)
    acc[...] = jnp.zeros_like(acc)
    row = lax.broadcasted_iota(jnp.int32, (blk, 1), 0)
    for j in range(2):
        n, local, src = ranked(slots, 0, j)

        @pl.when(n >= 0)
        def _():
            k, t = n // secs, n % secs
            live = live_columns(sizes, right_dims, src)
            for half, ref in ((h, own), (1 - h, own_far)):
                m_buf[pl.ds(pl.multiple_of(half * half_rows, half_rows), half_rows)] = ref[local] * live
            r = jnp.concatenate(
                [jnp.where(h == 0, right[k, t], right_far[k, t]), jnp.where(h == 0, right_far[k, t], right[k, t])],
                axis=0,
            )
            part = times_right(m_buf[...], r, row, left_dims[src])
            acc[t] += jnp.dot(left[k, t], part, preferred_element_type=F32)


class Late:
    def __init__(self, sizes, dims, side, left, right, right_far):
        self.sizes, self.dims, self.side = sizes, dims, side
        self.left, self.right, self.right_far = left, right, right_far
        z, self.o, self.h = place()
        self.mine = slots_of(sizes, dims[0], z, self.o)
        self.theirs = slots_of(sizes, dims[0], z, 1 - self.o)
        quarter = sizes[2] // 2
        self.halves = [self.h * sizes[2], (1 - self.h) * sizes[2]]
        self.ops = [self.o * quarter, (1 - self.o) * quarter]
        self.parts = []

    def target(self, n):
        n = jnp.maximum(n, 0)
        return n // self.sizes[1], n % self.sizes[1]

    def sided(self, mine, far):
        return jnp.where(self.side == self.h, mine, far)

    def add(self, slot, pieces, firsts, r, lefts):
        n, _, src = slot
        at = lax.broadcasted_iota(jnp.int32, (pieces[0].shape[0], 1), 0)
        row = jnp.concatenate([at + first for first in firsts], axis=0)
        left_live = jnp.where(n >= 0, self.dims[1][src], 0)
        live = live_columns(self.sizes, self.dims[2], src)
        part = times_right(jnp.concatenate(pieces, axis=0), r * live, row, left_live)
        self.parts.append((self.target(n)[1], jnp.concatenate(lefts, axis=1), part))

    def add_own(self, slot, pieces, firsts):
        k, t = self.target(slot[0])
        size = pieces[0].shape[0]
        lefts = [self.left[k, t, :, pl.ds(pl.multiple_of(first, size), size)] for first in firsts]
        self.add(slot, pieces, firsts, self.sided(self.right[k, t], self.right_far[k, t]), lefts)

    def add_near(self, near, near_far):
        for j in range(2):
            self.add_own(ranked(self.mine, 1, j), [near[j], near_far[j]], self.halves)

    def add_mid(self, mid, mid_x, mid_far, mid_x_far):
        for j in range(2):
            slot = ranked(self.mine, 2, j)
            pieces = [mid[slot[1]], mid_x[j], mid_far[slot[1]], mid_x_far[j]]
            self.add_own(slot, pieces, [half + op for half in self.halves for op in self.ops])

    def add_far(self, far, far_far, env_x, env_x_far):
        half_rows = self.sizes[2]
        quarter = half_rows // 2
        firsts = [half + self.ops[0] for half in self.halves]
        for j in range(2):
            slot = ranked(self.mine, 3, j)
            self.add_own(slot, [far[slot[1]], far_far[slot[1]]], firsts)
            slot = ranked(self.theirs, 3, j)
            lefts = [
                env_x[2, :, pl.ds(pl.multiple_of(j * half_rows + half * quarter, quarter), quarter)]
                for half in (self.h, 1 - self.h)
            ]
            r = self.sided(env_x[j], env_x_far[j])
            self.add(slot, [far[slot[1]], far_far[slot[1]]], firsts, r, lefts)

    def sum_into(self, total):
        for t, left, part in self.parts:
            total[t] += jnp.dot(left, part, preferred_element_type=F32)


def begin_kernel(kept, sizes, source, left_dims, right_dims, *refs):
    near, mid, envs, early, total = refs[:2], refs[2:6], refs[6:9], refs[9], refs[10]
    o = place()[1]
    side, half_rows = (o if kept else 1 - o), sizes[2]
    total[...] = early[:, :, pl.ds(pl.multiple_of(side * half_rows, half_rows), half_rows)]
    late = Late(sizes, (source, left_dims, right_dims), side, *envs)
    late.add_near(*near)
    late.add_mid(*mid)
    late.sum_into(total)


def finish_kernel(kept, sizes, source, left_dims, right_dims, *refs):
    fars, envs, total = refs[:4], refs[4:7], refs[8]
    o = place()[1]
    late = Late(sizes, (source, left_dims, right_dims), o if kept else 1 - o, *envs)
    late.add_far(*fars)
    late.sum_into(total)
    if not kept:
        refs[9][...] = total[...].astype(BF16)


def join_kernel(sizes, left_dims, right_dims, keep, received, out, held, sem):
    secs, half_rows, blk = sizes[1:]
    z, o, h = place()
    row = h * half_rows + lax.broadcasted_iota(jnp.int32, (half_rows, 1), 0)
    col = o * half_rows + lax.broadcasted_iota(jnp.int32, (1, half_rows), 1)
    copies = [pltpu.make_async_copy(held.at[t], out.at[t], sem.at[t]) for t in range(secs)]
    for t in range(secs):
        live = (row < left_dims[z * secs + t]) & (col < right_dims[z * secs + t])
        held[t] = jnp.where(live, keep[t] + received[t].astype(F32), 0.0).astype(BF16)
        copies[t].start()
    for copy in copies:
        copy.wait()


def swap(x, axis):
    return lax.ppermute(x, axis, [(0, 1), (1, 0)])


def after(x, *earlier):
    return lax.optimization_barrier((x, *earlier))[0]


def exchange(x, kind):
    return lax.ppermute(x, "sector", [(i, i ^ kind) for i in range(4)])


def four_by_two(wavefunction, left_env, right_env, source, left_dims, right_dims):
    secs, half_rows, blk = wavefunction.shape
    pairs = left_env.shape[0]
    quarter = half_rows // 2
    sizes = (pairs, secs, half_rows, blk)

    def call(
        kernel, name, outs, scalars, arrays, scratch=(), flops=0, space=pltpu.VMEM, limit=VMEM_LIMIT, to=pltpu.VMEM,
        aliases=None,
    ):
        shapes = [jax.ShapeDtypeStruct(shape, dtype) for shape, dtype in outs]
        nbytes = sum(s.size * s.dtype.itemsize for s in [*shapes, *arrays])
        return pl.pallas_call(
            functools.partial(kernel, sizes),
            out_shape=shapes,
            in_specs=[pl.BlockSpec(memory_space=pltpu.SMEM)] * len(scalars)
            + [pl.BlockSpec(memory_space=space)] * len(arrays),
            out_specs=[pl.BlockSpec(memory_space=to)] * len(shapes),
            scratch_shapes=scratch,
            compiler_params=pltpu.CompilerParams(vmem_limit_bytes=limit),
            cost_estimate=pl.CostEstimate(flops=flops, bytes_accessed=nbytes, transcendentals=0),
            name=name,
            input_output_aliases=aliases or {},
        )(*scalars, *arrays)

    dims = (source, left_dims, right_dims)
    share, near_out, env_out = call(
        first_kernel,
        "first",
        [((secs, quarter, blk), BF16), ((2, half_rows, blk), BF16), ((3, half_rows, blk), BF16)],
        (),
        (source, wavefunction, left_env, right_env),
        [
            pltpu.SMEM(source.shape, source.dtype),
            pltpu.VMEM((secs, half_rows, blk), BF16),
            pltpu.VMEM((2, half_rows, blk), BF16),
            pltpu.SemaphoreType.DMA((6,)),
        ],
        space=pltpu.HBM,
        limit=VMEM_MOST,
    )
    mid = exchange(share, 2)
    near = exchange(near_out, 1)
    env_x = swap(env_out, "op")
    own_far = swap(after(wavefunction, near_out), "half")
    right_far = swap(after(right_env, env_out), "half")
    loaded = (after(wavefunction, env_out), left_env, right_env)
    own, left, right = call(
        load_kernel,
        "load",
        [(x.shape, x.dtype) for x in loaded],
        (),
        loaded,
        [pltpu.SemaphoreType.DMA((3,))],
        flops=FILL,
        space=pltpu.HBM,
        limit=VMEM_MUCH,
    )
    mid, near, env_x, own_far, right_far = (after(x, own) for x in (mid, near, env_x, own_far, right_far))
    envs = (left, right, right_far)

    far = exchange(mid, 1)
    (picked,) = call(pick_kernel, "pick", [((2, quarter, blk), BF16)], (source,), (mid,))
    mid_x = swap(picked, "op")
    (early,) = call(
        own_kernel,
        "own_slots",
        [((secs, half_rows, blk), F32)],
        dims,
        (own, after(own_far, picked), *envs),
        [pltpu.VMEM((blk, blk), BF16)],
        flops=FILL,
    )
    mid_far = swap(after(mid, early), "half")
    mid_x, env_x = after(mid_x, early), after(env_x, early)
    mid_x_far = swap(mid_x, "half")
    env_x_far = swap(after(env_x[:2], early), "half")
    far = after(far, early, mid_x_far, mid_far)
    near = after(near, mid_x)
    arrivals = (near, swap(near, "half"), mid, mid_x, mid_far, mid_x_far)
    fars = (far, swap(far, "half"), env_x, env_x_far)
    columns = (secs, half_rows, half_rows)

    def side(kept, dtype, fill):
        (begun,) = call(
            functools.partial(begin_kernel, kept), "begin", [(columns, F32)], dims, (*arrivals, *envs, early), flops=fill
        )
        arrays = (*fars, *envs, begun)
        return call(
            functools.partial(finish_kernel, kept),
            "finish",
            [(columns, F32)] if kept else [(columns, F32), (columns, dtype)],
            dims,
            arrays,
            aliases={len(dims) + len(arrays) - 1: 0},
        )[-1]

    received = swap(side(False, BF16, 0), "op")
    keep = side(True, F32, 0)
    (out,) = call(
        join_kernel,
        "join",
        [(columns, BF16)],
        (left_dims, right_dims),
        (keep, received),
        [pltpu.VMEM(columns, BF16), pltpu.SemaphoreType.DMA((secs,))],
        to=pltpu.HBM,
    )
    return out


def solution(mesh):
    shape = mesh.shape
    fits = (shape["sector"], shape["op"], shape["half"]) == (4, 2, 2)
    return jax.shard_map(
        four_by_two if fits else general,
        mesh=mesh,
        in_specs=(
            P(("group", "sector"), "half", None),
            P("op", ("group", "sector"), "half", None),
            P("op", ("group", "sector"), "half", None),
            P(None, "group"),
            P("group"),
            P("group"),
        ),
        out_specs=P(("group", "sector"), "half", "op"),
        check_vma=False,
    )
```
